256 devices in a mesh: sec: 16 (over y, x), term: 16 (over z, core).
Axes of the slice: x: 4, y: 4, z: 8, core: 2. Of those that a mesh axis runs over, the one named last changes fastest.
Arguments:
- psi: bfloat16 [128, 384, 384], P('sec'), may hold values from -6 to 6
- left_env: bfloat16 [16, 2, 128, 384, 384], P('term', None, 'sec'), may hold values from -0.3125 to 0.3125
- right_env: bfloat16 [16, 2, 128, 384, 384], P('term', None, 'sec'), may hold values from -0.21875 to 0.21875
- targets: int32 [16, 128], P('term', 'sec'), may hold values from 0 to 127, as said below
- selected: int32 [16, 128], P('term', 'sec'), may hold values from 0 to 1, as said below
- block_dims: int32 [128, 2], P('sec'), may hold values from 192 to 384, as said below
Outputs:
- sigma: bfloat16 [128, 384, 384], P('sec', 'term')
The draws below stay inside these ranges and needn't reach their ends.
Inputs may be any that keep to these rules, and one draw needn't show every extreme that they name: For each term class w, targets[w] is a permutation of the 128 blocks. Blocks k and k2 belong to the same index of sec when k // 8 = k2 // 8; under one term class the blocks of one index of sec go to exactly 8 distinct indices of sec, exactly 1 block to each. Under each term class, between 1 and 6 of the 8 blocks of one index of sec are selected, exactly 6 on some index. `block_dims`: some block has both dimensions equal to 384.
All inputs are finite; a program needn't handle non-finite values.
Results may differ from the reference program's by a relative error of at most 0.013.
Values may be sent and summed in bfloat16 or wider, within the bound.
A program may use at most 64 MiB of HBM per device.

```python
import jax
import jax.numpy as jnp
from jax import lax

BS = 384
COMP = 2
NB_DEV = 8
SEL_DEV = 6
CAP = 1
NB = 128
TERMS = 16


def draw_targets(key, part):
    sec_total = NB // NB_DEV
    groups = min(NB_DEV, sec_total)
    key_off, key_src, key_dst = jax.random.split(key, 3)
    offsets = jax.vmap(lambda one_key: jax.random.permutation(one_key, sec_total)[:groups])(jax.random.split(key_off, TERMS))
    source_perm = jax.vmap(lambda one_key: jax.random.permutation(one_key, NB_DEV))(jax.random.split(key_src, TERMS * sec_total)).reshape(TERMS, sec_total, NB_DEV)
    dest_perm = jax.vmap(lambda one_key: jax.random.permutation(one_key, NB_DEV))(jax.random.split(key_dst, TERMS * sec_total)).reshape(TERMS, sec_total, NB_DEV)
    position = jnp.arange(NB_DEV, dtype=jnp.int32)
    group = position // CAP
    devices = jnp.arange(sec_total, dtype=jnp.int32)
    term_ids = jnp.arange(TERMS, dtype=jnp.int32)
    dest = (devices[None, :, None] + offsets[:, group][:, None, :]) % sec_total
    local_slot = dest_perm[term_ids[:, None, None], dest, position[None, None, :]]
    value = dest * NB_DEV + local_slot
    source_block = devices[None, :, None] * NB_DEV + source_perm
    term_grid = jnp.broadcast_to(term_ids[:, None, None], value.shape)
    result = jnp.zeros((TERMS, NB), jnp.int32).at[term_grid, source_block].set(value.astype(jnp.int32))
    return result.astype(jnp.int32)


def draw_selected(key, part):
    sec_total = NB // NB_DEV
    key_count, key_first, key_perm = jax.random.split(key, 3)
    counts = jax.random.randint(key_count, (TERMS, sec_total), 1, SEL_DEV + 1)
    first = jax.random.randint(key_first, (TERMS,), 0, sec_total)
    counts = jnp.where(jnp.arange(sec_total)[None, :] == first[:, None], SEL_DEV, counts)
    ranks = jax.vmap(lambda one_key: jax.random.permutation(one_key, NB_DEV))(jax.random.split(key_perm, TERMS * sec_total)).reshape(TERMS, sec_total, NB_DEV)
    chosen = (ranks < counts[:, :, None]).astype(jnp.int32)
    return chosen.reshape(TERMS, NB)


def draw_block_dims(key, part):
    key_dims, key_full = jax.random.split(key, 2)
    dims = jax.random.randint(key_dims, (NB, 2), BS // 2, BS + 1)
    full = jax.random.randint(key_full, (), 0, NB)
    dims = jnp.where(jnp.arange(NB)[:, None] == full, BS, dims)
    return dims.astype(jnp.int32)


def steps_of(rng, shape, cuts, smallest, top_value):
    factor_of = 1.0
    for dim, shards_of in cuts:
        steps = jax.random.uniform(jax.random.fold_in(jax.random.fold_in(rng, 6), dim), (shards_of,), jnp.float32, smallest / len(cuts), top_value / len(cuts))
        factor_of = factor_of * jnp.repeat(jnp.exp(steps), shape[dim] // shards_of).reshape((-1,) + (1,) * (len(shape) - 1 - dim))
    return factor_of


def normal_values(key, shape, scale, limit, cuts=(), kind=jnp.bfloat16):
    entries = jax.random.normal(key, shape, jnp.float32) * scale
    if len(cuts) > 0:
        entries = steps_of(key, shape, cuts, -0.22, 0.18) * entries
    return jnp.clip(entries, min=-limit, max=limit).astype(kind)


def setup_inputs(seed: int = 0) -> dict:
    splits = jax.random.split(jax.random.key(seed), 7)
    psi = normal_values(splits[0], (NB, BS, BS), 1.0, 6.0, ((0, 16),))
    left_env = normal_values(splits[1], (TERMS, COMP, NB, BS, BS), BS ** -0.5, 0.3125, ((0, 16), (2, 16)))
    right_env = normal_values(splits[2], (TERMS, COMP, NB, BS, BS), (COMP * BS) ** -0.5, 0.21875, ((0, 16), (2, 16)))
    targets = draw_targets(jax.random.fold_in(splits[6], 71), 0)
    selected = draw_selected(jax.random.fold_in(splits[6], 71), 0)
    block_dims = draw_block_dims(jax.random.fold_in(splits[6], 71), 0)
    return dict(psi=psi, left_env=left_env, right_env=right_env, targets=targets, selected=selected, block_dims=block_dims)


def reference(psi, left_env, right_env, targets, selected, block_dims):
    positions = jnp.arange(BS, dtype=jnp.int32)
    rows_ok = positions[None, :] < block_dims[:, 0:1]
    cols_ok = positions[None, :] < block_dims[:, 1:2]
    inside = rows_ok[:, :, None] & cols_ok[:, None, :]
    masked = jnp.where(inside, psi, jnp.zeros_like(psi))

    def one_term(summed, term_inputs):
        left_now, right_now, target, chosen = term_inputs
        half_product = jnp.einsum("mkab,kbc->mkac", left_now.astype(jnp.float32), masked.astype(jnp.float32)).astype(jnp.bfloat16)
        term_block = jnp.einsum("mkab,mkbc->kac", half_product.astype(jnp.float32), right_now.astype(jnp.float32))
        term_block = (term_block * chosen.astype(jnp.float32)[:, None, None]).astype(jnp.bfloat16)
        summed = summed.at[target.astype(jnp.int32)].add(term_block.astype(jnp.float32))
        return summed, None

    start = jnp.zeros((NB, BS, BS), jnp.float32)
    summed, unused = lax.scan(one_term, start, (left_env, right_env, targets, selected))
    return jnp.where(inside, summed, jnp.zeros_like(summed)).astype(jnp.bfloat16)
```

```python
import functools
import math

import jax
import jax.numpy as jnp
from jax import lax
from jax.experimental import pallas as pl
from jax.experimental.pallas import tpu as pltpu
from jax.sharding import PartitionSpec as P

MESH = pl.DeviceIdType.MESH
ITEMS = 6
COLS = 128
SUB = 8


def kernel(
    W, NY, NX,
    tgt, sel, dims, psi_h, left_h, right_h, out,
    psi_v, left_v, right_v, zsend, zrecv, msend, mrecv, onehot, ybuf,
    a1, b1, a2s, b2s, a2, b2, fin,
    load_sem, mesh_sems, zs_sem, zr_sem, s1_sem, r1_sem, s2_sem, r2_sem,
):
    w = lax.axis_index("term")
    s = lax.axis_index("sec")
    y, x = s // NX, s % NX
    NB, BS = psi_v.shape[0], psi_v.shape[1]
    C = BS // COLS
    rows = BS // W
    G = rows // SUB
    L = G * COLS
    R6 = ITEMS * SUB
    half = NB * SUB // 2
    pairs = ITEMS // 2
    K = W * R6

    loads = [(psi_h, psi_v)]
    for m in range(2):
        loads.append((left_h.at[0, m], left_v.at[m]))
        loads.append((right_h.at[0, m], right_v.at[m]))
    loads = [pltpu.make_async_copy(a, b, load_sem.at[n]) for n, (a, b) in enumerate(loads)]
    for copy in loads:
        copy.start()

    def z_peer(d):
        return lax.rem(w + d, W)

    def sec_at(yy, xx):
        return yy * NX + xx

    barrier = pltpu.get_barrier_semaphore()

    def greet(d, carry):
        pl.semaphore_signal(barrier, inc=1, device_id={"term": z_peer(d)}, device_id_type=MESH)
        return carry

    lax.fori_loop(1, W, greet, 0)
    for d in range(1, NY):
        pl.semaphore_signal(
            barrier, inc=1, device_id={"sec": sec_at(lax.rem(y + d, NY), x)}, device_id_type=MESH)
    for d in range(1, NX):
        pl.semaphore_signal(
            barrier, inc=1, device_id={"sec": sec_at(y, lax.rem(x + d, NX))}, device_id_type=MESH)

    chosen, ranks, count = [], [], jnp.int32(0)
    for k in range(NB):
        chosen.append(sel[0, k] != 0)
        ranks.append(count)
        count = count + jnp.where(chosen[k], 1, 0)

    def block_of(i):
        found = jnp.int32(0)
        for k in range(NB):
            found = found + jnp.where(chosen[k] & (ranks[k] == i), k, 0)
        return found

    lane = lax.broadcasted_iota(jnp.int32, (1, 128), 1)
    message = jnp.zeros((1, 128), jnp.int32)
    for i in range(ITEMS):
        place = jnp.int32(-1)
        for k in range(NB):
            place = place + jnp.where(chosen[k] & (ranks[k] == i), tgt[0, k] + 1, 0)
        value = jnp.where(place >= 0, place * SUB + lane % SUB + 1, 0)
        message = jnp.where(lane // SUB == i, value, message)
    msend[...] = message
    mrecv[w] = message

    pl.semaphore_wait(barrier, W - 1 + NY - 1 + NX - 1)

    def send_message(d, carry):
        pltpu.make_async_remote_copy(
            msend, mrecv.at[w], mesh_sems.at[0], mesh_sems.at[1],
            device_id={"term": z_peer(d)}, device_id_type=MESH).start()
        return carry

    lax.fori_loop(1, W, send_message, 0)

    def send_z(c, first, size, piece):
        part = pl.ds(first, size)

        def one(d, carry):
            peer = z_peer(d)
            pltpu.make_async_remote_copy(
                zsend.at[c, peer, part], zrecv.at[c, w, part], zs_sem.at[piece], zr_sem.at[piece],
                device_id={"term": peer}, device_id_type=MESH).start()
            return carry

        lax.fori_loop(1, W, one, 0)

    def wait_for(ref, sem):
        pltpu.make_async_copy(ref, ref, sem).wait()

    for copy in loads:
        copy.wait()

    row_id = lax.broadcasted_iota(jnp.int32, (BS, BS), 0)
    col_id = lax.broadcasted_iota(jnp.int32, (BS, BS), 1)

    def one_block(i):
        k = block_of(i)
        block = psi_v[k]
        keep = (row_id < dims[k, 0]) & (col_id < dims[k, 1])
        block = jnp.where(keep, block, jnp.zeros_like(block))
        total = None
        for m in range(2):
            half_product = jnp.dot(left_v[m, k], block, preferred_element_type=jnp.float32)
            term = jnp.dot(
                half_product.astype(jnp.bfloat16), right_v[m, k], preferred_element_type=jnp.float32)
            total = term if total is None else total + term
        return total.reshape(W * G, SUB, BS)

    def one_pair(p, carry):
        both = jnp.concatenate([one_block(2 * p), one_block(2 * p + 1)], axis=1).astype(jnp.bfloat16)
        both = both.reshape(W, G, 2 * SUB, BS)
        first = pl.multiple_of(p * 2 * SUB, 2 * SUB)
        for c in range(C):
            for g in range(G):
                zsend[c, :, pl.ds(first, 2 * SUB), g * COLS:(g + 1) * COLS] = (
                    both[:, g, :, c * COLS:(c + 1) * COLS])
        send_z(0, first, 2 * SUB, p)
        return carry

    lax.fori_loop(0, pairs, one_pair, 0)
    for c in range(1, C):
        send_z(c, 0, R6, pairs - 1 + c)
    for c in range(C):
        zrecv[c, w] = zsend[c, w]

    wait_for(mrecv.at[pl.ds(0, W - 1)], mesh_sems.at[1])
    width = -(-K // 128) * 128
    places = jnp.zeros((2 * SUB, width), jnp.int32)
    for n in range(W):
        wide = jnp.broadcast_to(mrecv[n], (2 * SUB, 128))
        if width > 128:
            wide = jnp.concatenate([wide, jnp.zeros((2 * SUB, width - 128), jnp.int32)], axis=1)
        places = places + (pltpu.roll(wide, n * R6, 1) if n else wide)
    places = places[:, :K]
    step = lax.broadcasted_iota(jnp.int32, (2 * SUB, K), 0) + 1

    def fill(b, carry):
        first = pl.multiple_of(b * 2 * SUB, 2 * SUB)
        onehot[pl.ds(first, 2 * SUB), :] = jnp.where(
            places == step + first, 1.0, 0.0).astype(jnp.bfloat16)
        return carry

    lax.fori_loop(0, NY * NX * NB * SUB // (2 * SUB), fill, 0)

    block_rows = NX * NB * SUB
    for c in range(C):
        if c == 0:
            for p in range(pairs):
                wait_for(zrecv.at[0, pl.ds(0, W - 1), pl.ds(p * 2 * SUB, 2 * SUB)], zr_sem.at[p])
        else:
            wait_for(zrecv.at[c, pl.ds(0, W - 1)], zr_sem.at[pairs - 1 + c])
        arrived = zrecv[c].reshape(K, L)
        for yy in range(NY):
            part = jnp.dot(
                onehot[yy * block_rows:(yy + 1) * block_rows, :], arrived,
                preferred_element_type=jnp.float32)
            ybuf[c, yy] = part.astype(jnp.bfloat16).reshape(NX, NB * SUB, L)
        for d in range(1, NY):
            yy = lax.rem(y + d, NY)
            pltpu.make_async_remote_copy(
                ybuf.at[c, yy, :, pl.ds(0, half)], a1.at[c, d - 1], s1_sem.at[0, c], r1_sem.at[0, c],
                device_id={"sec": sec_at(yy, x)}, device_id_type=MESH).start()
        for d in range(1, NX):
            xx = lax.rem(x + d, NX)
            pltpu.make_async_remote_copy(
                ybuf.at[c, :, xx, pl.ds(half, half)], b1.at[c, d - 1], s1_sem.at[1, c], r1_sem.at[1, c],
                device_id={"sec": sec_at(y, xx)}, device_id_type=MESH).start()

        wait_for(a1.at[c], r1_sem.at[0, c])
        total = ybuf[c, y, :, :half, :].astype(jnp.float32)
        for n in range(NY - 1):
            total = total + a1[c, n].astype(jnp.float32)
        a2s[c] = total.astype(jnp.bfloat16)
        for d in range(1, NX):
            xx = lax.rem(x + d, NX)
            pltpu.make_async_remote_copy(
                a2s.at[c, xx], a2.at[c, d - 1], s2_sem.at[0, c], r2_sem.at[0, c],
                device_id={"sec": sec_at(y, xx)}, device_id_type=MESH).start()
        wait_for(b1.at[c], r1_sem.at[1, c])
        total = ybuf[c, :, x, half:, :].astype(jnp.float32)
        for n in range(NX - 1):
            total = total + b1[c, n].astype(jnp.float32)
        b2s[c] = total.astype(jnp.bfloat16)
        for d in range(1, NY):
            yy = lax.rem(y + d, NY)
            pltpu.make_async_remote_copy(
                b2s.at[c, yy], b2.at[c, d - 1], s2_sem.at[1, c], r2_sem.at[1, c],
                device_id={"sec": sec_at(yy, x)}, device_id_type=MESH).start()

        wait_for(a2.at[c], r2_sem.at[0, c])
        wait_for(b2.at[c], r2_sem.at[1, c])
        for own, others, place, at in ((a2s, a2, x, 0), (b2s, b2, y, NB // 2)):
            total = own[c, place].astype(jnp.float32)
            for n in range(others.shape[1]):
                total = total + others[c, n].astype(jnp.float32)
            for g in range(G):
                fin[at:at + NB // 2, g * SUB:(g + 1) * SUB, c * COLS:(c + 1) * COLS] = (
                    total[:, g * COLS:(g + 1) * COLS].reshape(NB // 2, SUB, COLS))

    row_id = lax.broadcasted_iota(jnp.int32, (rows, BS), 0) + w * rows
    col_id = lax.broadcasted_iota(jnp.int32, (rows, BS), 1)
    for j in range(NB):
        keep = (row_id < dims[j, 0]) & (col_id < dims[j, 1])
        out[j] = jnp.where(keep, fin[j], 0.0).astype(out.dtype)

    for _ in range(1):
        wait_for(mrecv.at[pl.ds(0, W - 1)], mesh_sems.at[0])
    for p in range(pairs):
        wait_for(zsend.at[0, pl.ds(0, W - 1), pl.ds(p * 2 * SUB, 2 * SUB)], zs_sem.at[p])
    for c in range(1, C):
        wait_for(zsend.at[c, pl.ds(0, W - 1)], zs_sem.at[pairs - 1 + c])
    for c in range(C):
        wait_for(a1.at[c], s1_sem.at[0, c])
        wait_for(b1.at[c], s1_sem.at[1, c])
        wait_for(a2.at[c], s2_sem.at[0, c])
        wait_for(b2.at[c], s2_sem.at[1, c])


def shards(W, SEC, psi, left_env, right_env, targets, selected, block_dims):
    NB, BS, _ = psi.shape
    NX = math.isqrt(SEC)
    NY = SEC // NX
    C = BS // COLS
    rows = BS // W
    G = rows // SUB
    L = G * COLS
    R6 = ITEMS * SUB
    half = NB * SUB // 2
    bf16, f32, i32 = jnp.bfloat16, jnp.float32, jnp.int32
    dma = pltpu.SemaphoreType.DMA
    smem = pl.BlockSpec(memory_space=pltpu.SMEM)
    anyspace = pl.BlockSpec(memory_space=pl.ANY)
    pieces = ITEMS // 2 + C - 1
    return pl.pallas_call(
        functools.partial(kernel, W, NY, NX),
        out_shape=jax.ShapeDtypeStruct((NB, rows, BS), bf16),
        in_specs=[smem, smem, smem, anyspace, anyspace, anyspace],
        out_specs=pl.BlockSpec(memory_space=pltpu.VMEM),
        scratch_shapes=[
            pltpu.VMEM((NB, BS, BS), bf16),
            pltpu.VMEM((2, NB, BS, BS), bf16),
            pltpu.VMEM((2, NB, BS, BS), bf16),
            pltpu.VMEM((C, W, R6, L), bf16),
            pltpu.VMEM((C, W, R6, L), bf16),
            pltpu.VMEM((1, 128), i32),
            pltpu.VMEM((W, 1, 128), i32),
            pltpu.VMEM((SEC * NB * SUB, W * R6), bf16),
            pltpu.VMEM((C, NY, NX, NB * SUB, L), bf16),
            pltpu.VMEM((C, NY - 1, NX, half, L), bf16),
            pltpu.VMEM((C, NX - 1, NY, half, L), bf16),
            pltpu.VMEM((C, NX, half, L), bf16),
            pltpu.VMEM((C, NY, half, L), bf16),
            pltpu.VMEM((C, NX - 1, half, L), bf16),
            pltpu.VMEM((C, NY - 1, half, L), bf16),
            pltpu.VMEM((NB, rows, BS), f32),
            dma((5,)), dma((2,)), dma((pieces,)), dma((pieces,)),
            dma((2, C)), dma((2, C)), dma((2, C)), dma((2, C)),
        ],
        compiler_params=pltpu.CompilerParams(
            collective_id=0, has_side_effects=True, vmem_limit_bytes=48 * 2**20),
        cost_estimate=pl.CostEstimate(flops=8 * 10**9, bytes_accessed=12 * 10**6, transcendentals=0),
        name="davidson",
    )(targets, selected, block_dims, psi, left_env, right_env)


def solution(mesh):
    W, SEC = mesh.shape["term"], mesh.shape["sec"]
    return jax.shard_map(
        functools.partial(shards, W, SEC),
        mesh=mesh,
        in_specs=(
            P("sec", None, None),
            P("term", None, "sec", None, None),
            P("term", None, "sec", None, None),
            P("term", "sec"),
            P("term", "sec"),
            P("sec", None),
        ),
        out_specs=P("sec", "term", None),
        check_vma=False,
    )
```

```python
import functools
import math

import jax
import jax.numpy as jnp
from jax import lax
from jax.experimental import pallas as pl
from jax.experimental.pallas import tpu as pltpu
from jax.sharding import PartitionSpec as P

MESH = pl.DeviceIdType.MESH
ITEMS = 6
COLS = 128
SUB = 8
XG = 2


def kernel(
    W, NY, NX,
    tgt_h, sel_h, dims_h, psi_h, left_h, right_h, out,
    tgt, sel, dims, psi_v, left_v, right_v, zsend, zrecv, msend, mrecv, onehot, ybuf,
    a1, b1, a2s, b2s, a2, b2, fin,
    xmsend, xmrecv, xitems, xsend, xrecv, xhot, xplaced, xcore, xsum, xlast,
    int_sem, load_sem, mesh_sems, zs_sem, zr_sem, s1_sem, r1_sem, s2_sem, r2_sem, xs_sem, xr_sem,
):
    w = lax.axis_index("term")
    s = lax.axis_index("sec")
    y, x = s // NX, s % NX
    NB, BS = psi_v.shape[0], psi_v.shape[1]
    rows = BS // W
    G = rows // SUB
    C = BS // COLS * G - XG
    R6 = ITEMS * SUB
    half = NB * SUB // 2
    pairs = ITEMS // 2
    K = W * R6
    SEC = NY * NX
    z, core = w // 2, w % 2

    ints = [(tgt_h, tgt), (sel_h, sel), (dims_h, dims)]
    ints = [pltpu.make_async_copy(a, b, int_sem.at[n]) for n, (a, b) in enumerate(ints)]
    for copy in ints:
        copy.start()
    loads = [(psi_h, psi_v)]
    for m in range(2):
        loads.append((left_h.at[0, m], left_v.at[:, m]))
    for m in range(2):
        loads.append((right_h.at[0, m], right_v.at[:, m]))
    loads = [pltpu.make_async_copy(a, b, load_sem.at[n]) for n, (a, b) in enumerate(loads)]
    for copy in loads:
        copy.start()

    def z_peer(d):
        return lax.rem(w + d, W)

    def sec_at(yy, xx):
        return yy * NX + xx

    barrier = pltpu.get_barrier_semaphore()

    def greet(d, carry):
        pl.semaphore_signal(barrier, inc=1, device_id={"term": z_peer(d)}, device_id_type=MESH)
        return carry

    lax.fori_loop(1, W, greet, 0)
    def greet_sec(d, carry):
        pl.semaphore_signal(
            barrier, inc=1, device_id={"sec": lax.rem(s + d, SEC)}, device_id_type=MESH)
        return carry

    lax.fori_loop(1, SEC, greet_sec, 0)

    for copy in ints:
        copy.wait()
    chosen, ranks, owners, slots, count = [], [], [], [], jnp.int32(0)
    for k in range(NB):
        chosen.append(sel[0, k] != 0)
        owners.append(lax.div(tgt[0, k], NB))
        slots.append(lax.rem(tgt[0, k], NB))
        ranks.append(count)
        count = count + jnp.where(chosen[k], 1, 0)

    def block_of(i):
        found = jnp.int32(0)
        for k in range(NB):
            found = found + jnp.where(chosen[k] & (ranks[k] == i), k, 0)
        return found

    lane = lax.broadcasted_iota(jnp.int32, (1, 128), 1)
    message = jnp.zeros((1, 128), jnp.int32)
    for i in range(ITEMS):
        place = jnp.int32(-1)
        for k in range(NB):
            place = place + jnp.where(chosen[k] & (ranks[k] == i), tgt[0, k] + 1, 0)
        value = jnp.where(place >= 0, place * SUB + lane % SUB + 1, 0)
        message = jnp.where(lane // SUB == i, value, message)
    msend[...] = message
    mrecv[w] = message

    item_of, slot_of = [], []
    for t in range(SEC):
        item, slot = jnp.int32(0), jnp.int32(0)
        for k in range(NB):
            hit = chosen[k] & (owners[k] == t)
            item = item + jnp.where(hit, ranks[k], 0)
            slot = slot + jnp.where(hit, slots[k] + 1, 0)
        item_of.append(item)
        slot_of.append(slot)
        xmsend[t] = jnp.zeros((1, 128), jnp.int32) + slot
    xmrecv[s] = xmsend[s]

    pl.semaphore_wait(barrier, W - 1 + SEC - 1)

    def send_message(d, carry):
        pltpu.make_async_remote_copy(
            msend, mrecv.at[w], mesh_sems.at[0], mesh_sems.at[1],
            device_id={"term": z_peer(d)}, device_id_type=MESH).start()
        return carry

    lax.fori_loop(1, W, send_message, 0)

    def send_slot(d, carry):
        peer = lax.rem(s + d, SEC)
        pltpu.make_async_remote_copy(
            xmsend.at[peer], xmrecv.at[s], xs_sem.at[0], xr_sem.at[0],
            device_id={"sec": peer}, device_id_type=MESH).start()
        return carry

    lax.fori_loop(1, SEC, send_slot, 0)

    def wait_for(ref, sem):
        pltpu.make_async_copy(ref, ref, sem).wait()

    for copy in loads:
        copy.wait()

    row_id = lax.broadcasted_iota(jnp.int32, (BS, BS), 0)
    col_id = lax.broadcasted_iota(jnp.int32, (BS, BS), 1)

    def one_block(i):
        k = block_of(i)
        block = psi_v[k]
        keep = (row_id < dims[0, k]) & (col_id < dims[1, k])
        block = jnp.where(keep, block, jnp.zeros_like(block))
        half_product = jnp.dot(
            left_v[k].reshape(2 * BS, BS), block, preferred_element_type=jnp.float32
        ).astype(jnp.bfloat16)
        half_product = jnp.concatenate([half_product[:BS], half_product[BS:]], axis=1)
        total = jnp.dot(
            half_product, right_v[k].reshape(2 * BS, BS), preferred_element_type=jnp.float32)
        return total.reshape(W * G, SUB, BS)

    def one_pair(p, carry):
        both = []
        for e in range(2):
            block = one_block(2 * p + e)
            both.append(block)
            last = block.reshape(W, G, SUB, BS)[:, G - XG:, :, BS - COLS:]
            xitems[2 * p + e] = last.reshape(W * XG // 2, 2 * SUB, COLS).astype(jnp.bfloat16)
        both = jnp.concatenate(both, axis=1).astype(jnp.bfloat16).reshape(W, G, 2 * SUB, BS)
        part = pl.ds(pl.multiple_of(p * 2 * SUB, 2 * SUB), 2 * SUB)
        for c in range(C):
            at = c // G * COLS
            zsend[c, :, part, :] = both[:, c % G, :, at:at + COLS]

        def one(d, carry):
            peer = z_peer(d)
            pltpu.make_async_remote_copy(
                zsend.at[pl.ds(0, G), peer, part], zrecv.at[pl.ds(0, G), w, part],
                zs_sem.at[p], zr_sem.at[p],
                device_id={"term": peer}, device_id_type=MESH).start()
            return carry

        lax.fori_loop(1, W, one, 0)
        return carry

    lax.fori_loop(0, pairs, one_pair, 0)

    def send_chunk(c, carry):
        def one(d, carry):
            peer = z_peer(d)
            pltpu.make_async_remote_copy(
                zsend.at[c, peer], zrecv.at[c, w], zs_sem.at[pairs + c], zr_sem.at[pairs + c],
                device_id={"term": peer}, device_id_type=MESH).start()
            return carry

        return lax.fori_loop(1, W, one, carry)


    for t in range(SEC):
        xsend[t] = jnp.where(slot_of[t] > 0, xitems[item_of[t]], jnp.zeros(xsend.shape[1:], jnp.bfloat16))

    def send_item(d, carry):
        peer = lax.rem(s + d, SEC)
        pltpu.make_async_remote_copy(
            xsend.at[peer], xrecv.at[:, s], xs_sem.at[1], xr_sem.at[1],
            device_id={"sec": peer}, device_id_type=MESH).start()
        return carry

    lax.fori_loop(1, SEC, send_item, 0)
    lax.fori_loop(G, C, send_chunk, 0)
    xrecv[:, s] = xsend[s]
    for c in range(C):
        zrecv[c, w] = zsend[c, w]

    wait_for(xmrecv.at[pl.ds(0, SEC - 1)], xr_sem.at[0])
    wide = -(-SEC * 2 * SUB // 128)
    lane = lax.broadcasted_iota(jnp.int32, (1, wide * 128), 1)
    slot = jnp.zeros((1, wide * 128), jnp.int32)
    for n in range(SEC):
        slot = jnp.where(lane // (2 * SUB) == n, jnp.concatenate([xmrecv[n]] * wide, axis=1), slot)
    place = (slot - 1) * SUB + lane % (2 * SUB) // SUB * (NB * SUB) + lane % SUB
    place = jnp.where(slot > 0, place, -1)[:, :SEC * 2 * SUB]
    row = lax.broadcasted_iota(jnp.int32, xhot.shape, 0)
    xhot[...] = jnp.where(row == place, 1.0, 0.0).astype(jnp.bfloat16)

    wait_for(mrecv.at[pl.ds(0, W - 1)], mesh_sems.at[1])
    width = -(-K // 128) * 128
    places = jnp.zeros((2 * SUB, width), jnp.int32)
    for n in range(W):
        wide = jnp.broadcast_to(mrecv[n], (2 * SUB, 128))
        if width > 128:
            wide = jnp.concatenate([wide, jnp.zeros((2 * SUB, width - 128), jnp.int32)], axis=1)
        places = places + (pltpu.roll(wide, n * R6, 1) if n else wide)
    places = places[:, :K]
    step = lax.broadcasted_iota(jnp.int32, (2 * SUB, K), 0) + 1

    def fill(b, carry):
        first = pl.multiple_of(b * 2 * SUB, 2 * SUB)
        onehot[pl.ds(first, 2 * SUB), :] = jnp.where(
            places == step + first, 1.0, 0.0).astype(jnp.bfloat16)
        return carry

    lax.fori_loop(0, NY * NX * NB * SUB // (2 * SUB), fill, 0)

    block_rows = NX * NB * SUB

    def by_target(c):
        @pl.when(c == 0)
        def _():
            for p in range(pairs):
                part = pl.ds(p * 2 * SUB, 2 * SUB)
                wait_for(zrecv.at[pl.ds(0, G), pl.ds(0, W - 1), part], zr_sem.at[p])

        @pl.when(c >= G)
        def _():
            wait_for(zrecv.at[c, pl.ds(0, W - 1)], zr_sem.at[pairs + c])

        arrived = zrecv[c].reshape(K, COLS)
        for yy in range(NY):
            part = jnp.dot(
                onehot[yy * block_rows:(yy + 1) * block_rows, :], arrived,
                preferred_element_type=jnp.float32)
            ybuf[c, yy] = part.astype(jnp.bfloat16).reshape(NX, NB * SUB, COLS)
        for d in range(1, NY):
            yy = lax.rem(y + d, NY)
            pltpu.make_async_remote_copy(
                ybuf.at[c, yy, :, pl.ds(0, half)], a1.at[c, d - 1], s1_sem.at[0, c], r1_sem.at[0, c],
                device_id={"sec": sec_at(yy, x)}, device_id_type=MESH).start()
        for d in range(1, NX):
            xx = lax.rem(x + d, NX)
            pltpu.make_async_remote_copy(
                ybuf.at[c, :, xx, pl.ds(half, half)], b1.at[c, d - 1], s1_sem.at[1, c], r1_sem.at[1, c],
                device_id={"sec": sec_at(y, xx)}, device_id_type=MESH).start()

    def one_axis(c):
        wait_for(a1.at[c], r1_sem.at[0, c])
        total = ybuf[c, y, :, :half, :].astype(jnp.float32)
        for n in range(NY - 1):
            total = total + a1[c, n].astype(jnp.float32)
        a2s[c] = total.astype(jnp.bfloat16)
        for d in range(1, NX):
            xx = lax.rem(x + d, NX)
            pltpu.make_async_remote_copy(
                a2s.at[c, xx], a2.at[c, d - 1], s2_sem.at[0, c], r2_sem.at[0, c],
                device_id={"sec": sec_at(y, xx)}, device_id_type=MESH).start()
        wait_for(b1.at[c], r1_sem.at[1, c])
        total = ybuf[c, :, x, half:, :].astype(jnp.float32)
        for n in range(NX - 1):
            total = total + b1[c, n].astype(jnp.float32)
        b2s[c] = total.astype(jnp.bfloat16)
        for d in range(1, NY):
            yy = lax.rem(y + d, NY)
            pltpu.make_async_remote_copy(
                b2s.at[c, yy], b2.at[c, d - 1], s2_sem.at[1, c], r2_sem.at[1, c],
                device_id={"sec": sec_at(yy, x)}, device_id_type=MESH).start()

    def other_axis(c):
        wait_for(a2.at[c], r2_sem.at[0, c])
        wait_for(b2.at[c], r2_sem.at[1, c])
        for own, others, place, at in ((a2s, a2, x, 0), (b2s, b2, y, half)):
            total = own[c, place].astype(jnp.float32)
            for n in range(others.shape[1]):
                total = total + others[c, n].astype(jnp.float32)
            fin[c, at:at + half, :] = total

    def place_items():
        wait_for(xrecv.at[:, pl.ds(0, SEC - 1)], xr_sem.at[1])
        for n in range(W * XG // 2):
            part = jnp.dot(
                xhot[...], xrecv[n].reshape(SEC * 2 * SUB, COLS), preferred_element_type=jnp.float32
            ).astype(jnp.bfloat16)
            for e in range(2):
                at = 2 * n + e
                to, first = at // XG, at % XG * NB * SUB
                xplaced[to % 2, to // 2, first:first + NB * SUB, :] = part[e * NB * SUB:(e + 1) * NB * SUB]
        pltpu.make_async_remote_copy(
            xplaced.at[1 - core], xcore, xs_sem.at[2], xr_sem.at[2],
            device_id={"term": w + 1 - 2 * core}, device_id_type=MESH).start()

    def add_cores():
        wait_for(xcore, xr_sem.at[2])
        xsum[...] = (xplaced[core].astype(jnp.float32) + xcore[...].astype(jnp.float32)).astype(jnp.bfloat16)
        for d in range(1, W // 2):
            peer = lax.rem(z + d, W // 2)
            pltpu.make_async_remote_copy(
                xsum.at[peer], xlast.at[d - 1], xs_sem.at[3], xr_sem.at[3],
                device_id={"term": peer * 2 + core}, device_id_type=MESH).start()

    def step_of(t, carry):
        @pl.when(t == G + 1)
        def _():
            place_items()

        @pl.when(t == G + 2)
        def _():
            add_cores()

        @pl.when(t < C)
        def _():
            by_target(t)

        @pl.when((t >= 1) & (t <= C))
        def _():
            one_axis(t - 1)

        @pl.when(t >= 2)
        def _():
            other_axis(t - 2)

        return carry

    lax.fori_loop(0, C + 2, step_of, 0)

    wait_for(xlast, xr_sem.at[3])
    total = xsum[z].astype(jnp.float32)
    for n in range(W // 2 - 1):
        total = total + xlast[n].astype(jnp.float32)
    fin[C:] = total.reshape(XG, NB * SUB, COLS)

    row_id = lax.broadcasted_iota(jnp.int32, (rows, BS), 0) + w * rows
    col_id = lax.broadcasted_iota(jnp.int32, (rows, BS), 1)
    for j in range(NB):
        keep = (row_id < dims[0, j]) & (col_id < dims[1, j])
        total = jnp.concatenate([
            jnp.concatenate([
                fin[q * G + g, j * SUB:(j + 1) * SUB, :] for q in range(BS // COLS)], axis=1)
            for g in range(G)], axis=0)
        out[j] = jnp.where(keep, total, 0.0).astype(out.dtype)

    wait_for(mrecv.at[pl.ds(0, W - 1)], mesh_sems.at[0])
    for p in range(pairs):
        part = pl.ds(p * 2 * SUB, 2 * SUB)
        wait_for(zsend.at[pl.ds(0, G), pl.ds(0, W - 1), part], zs_sem.at[p])

    def sent(c, carry):
        @pl.when(c >= G)
        def _():
            wait_for(zsend.at[c, pl.ds(0, W - 1)], zs_sem.at[pairs + c])

        wait_for(a1.at[c], s1_sem.at[0, c])
        wait_for(b1.at[c], s1_sem.at[1, c])
        wait_for(a2.at[c], s2_sem.at[0, c])
        wait_for(b2.at[c], s2_sem.at[1, c])
        return carry

    lax.fori_loop(0, C, sent, 0)
    wait_for(xmrecv.at[pl.ds(0, SEC - 1)], xs_sem.at[0])
    wait_for(xsend.at[pl.ds(0, SEC - 1)], xs_sem.at[1])
    wait_for(xcore, xs_sem.at[2])
    wait_for(xlast, xs_sem.at[3])


def shards(W, SEC, psi, left_env, right_env, targets, selected, block_dims):
    NB, BS, _ = psi.shape
    NX = math.isqrt(SEC)
    NY = SEC // NX
    rows = BS // W
    C = BS // COLS * (rows // SUB) - XG
    pairs_here = W * XG // 2
    R6 = ITEMS * SUB
    half = NB * SUB // 2
    bf16, f32, i32 = jnp.bfloat16, jnp.float32, jnp.int32
    dma = pltpu.SemaphoreType.DMA
    hbm = pl.BlockSpec(memory_space=pltpu.HBM)
    return pl.pallas_call(
        functools.partial(kernel, W, NY, NX),
        out_shape=pltpu.VMEM((NB, rows, BS), bf16),
        in_specs=[hbm] * 6,
        out_specs=pl.BlockSpec(memory_space=pltpu.VMEM),
        scratch_shapes=[
            pltpu.SMEM((1, NB), i32),
            pltpu.SMEM((1, NB), i32),
            pltpu.SMEM((2, NB), i32),
            pltpu.VMEM((NB, BS, BS), bf16),
            pltpu.VMEM((NB, 2, BS, BS), bf16),
            pltpu.VMEM((NB, 2, BS, BS), bf16),
            pltpu.VMEM((C, W, R6, COLS), bf16),
            pltpu.VMEM((C, W, R6, COLS), bf16),
            pltpu.VMEM((1, 128), i32),
            pltpu.VMEM((W, 1, 128), i32),
            pltpu.VMEM((SEC * NB * SUB, W * R6), bf16),
            pltpu.VMEM((C, NY, NX, NB * SUB, COLS), bf16),
            pltpu.VMEM((C, NY - 1, NX, half, COLS), bf16),
            pltpu.VMEM((C, NX - 1, NY, half, COLS), bf16),
            pltpu.VMEM((C, NX, half, COLS), bf16),
            pltpu.VMEM((C, NY, half, COLS), bf16),
            pltpu.VMEM((C, NX - 1, half, COLS), bf16),
            pltpu.VMEM((C, NY - 1, half, COLS), bf16),
            pltpu.VMEM((C + XG, NB * SUB, COLS), f32),
            pltpu.VMEM((SEC, 1, 128), i32),
            pltpu.VMEM((SEC, 1, 128), i32),
            pltpu.VMEM((ITEMS, pairs_here, 2 * SUB, COLS), bf16),
            pltpu.VMEM((SEC, pairs_here, 2 * SUB, COLS), bf16),
            pltpu.VMEM((pairs_here, SEC, 2 * SUB, COLS), bf16),
            pltpu.VMEM((2 * NB * SUB, SEC * 2 * SUB), bf16),
            pltpu.VMEM((2, W // 2, XG * NB * SUB, COLS), bf16),
            pltpu.VMEM((W // 2, XG * NB * SUB, COLS), bf16),
            pltpu.VMEM((W // 2, XG * NB * SUB, COLS), bf16),
            pltpu.VMEM((W // 2 - 1, XG * NB * SUB, COLS), bf16),
            dma((3,)), dma((5,)), dma((2,)), dma((ITEMS // 2 + C,)), dma((ITEMS // 2 + C,)),
            dma((2, C)), dma((2, C)), dma((2, C)), dma((2, C)), dma((4,)), dma((4,)),
        ],
        compiler_params=pltpu.CompilerParams(
            collective_id=0, has_side_effects=True, vmem_limit_bytes=54 * 2**20),
        cost_estimate=pl.CostEstimate(flops=8 * 10**9, bytes_accessed=12 * 10**6, transcendentals=0),
        name="davidson",
    )(targets, selected, block_dims.T, psi, left_env, right_env)


def solution(mesh):
    W, SEC = mesh.shape["term"], mesh.shape["sec"]
    return jax.shard_map(
        functools.partial(shards, W, SEC),
        mesh=mesh,
        in_specs=(
            P("sec", None, None),
            P("term", None, "sec", None, None),
            P("term", None, "sec", None, None),
            P("term", "sec"),
            P("term", "sec"),
            P("sec", None),
        ),
        out_specs=P("sec", "term", None),
        check_vma=False,
    )
```

```python
import functools
import math

import jax
import jax.numpy as jnp
from jax import lax
from jax.experimental import pallas as pl
from jax.experimental.pallas import tpu as pltpu
from jax.sharding import PartitionSpec as P

MESH = pl.DeviceIdType.MESH
ITEMS = 6
COLS = 128
SUB = 8
XG = 2


def kernel(
    W, NY, NX,
    tgt_h, sel_h, dims_h, psi_h, left_h, right_h, out,
    tgt, sel, dims, psi_v, left_v, right_v, rest_v, halves, zsend, zrecv, msend, mrecv, onehot, ybuf,
    a1, b1, a2s, b2s, a2, b2, fin,
    direct, xmsend, xmrecv, xitems, xsend, xrecv, xhot, xplaced, xcore, xsum, xlast,
    int_sem, load_sem, mesh_sems, zs_sem, zr_sem, s1_sem, r1_sem, s2_sem, r2_sem, xs_sem, xr_sem, d_sem,
):
    w = lax.axis_index("term")
    s = lax.axis_index("sec")
    y, x = s // NX, s % NX
    NB, BS = psi_v.shape[0], psi_v.shape[1]
    rows = BS // W
    G = rows // SUB
    C = BS // COLS * G - XG
    R6 = ITEMS * SUB
    half = NB * SUB // 2
    pairs = ITEMS // 2
    K = W * R6
    SEC = NY * NX
    z, core = w // 2, w % 2

    ints = [(tgt_h, tgt), (sel_h, sel), (dims_h, dims)]
    ints = [pltpu.make_async_copy(a, b, int_sem.at[n]) for n, (a, b) in enumerate(ints)]
    for copy in ints:
        copy.start()
    loads = [(psi_h, psi_v)]
    for m in range(2):
        loads.append((left_h.at[0, m], left_v.at[:, m]))
    for m in range(2):
        loads.append((right_h.at[0, m, :, :, pl.ds(0, COLS)], right_v.at[:, m]))
    for m in range(2):
        loads.append((right_h.at[0, m, :, :, pl.ds(COLS, BS - COLS)], rest_v.at[:, m]))
    loads = [pltpu.make_async_copy(a, b, load_sem.at[n]) for n, (a, b) in enumerate(loads)]
    for copy in loads[:5]:
        copy.start()

    def z_peer(d):
        return lax.rem(w + d, W)

    def far(d, n):
        return -min(d, n - d)

    z_turns = sorted(((d, c) for d in range(1, W // 2) for c in range(2)), key=lambda t: far(t[0], W // 2))
    z_turns = [(0, 1)] + z_turns
    turns = [(dy, dx) for dy in range(NY) for dx in range(NX) if dy or dx]
    turns = sorted(turns, key=lambda t: far(t[0], NY) + far(t[1], NX))

    def sec_at(yy, xx):
        return yy * NX + xx

    barrier = pltpu.get_barrier_semaphore()

    def greet(d, carry):
        pl.semaphore_signal(barrier, inc=1, device_id={"term": z_peer(d)}, device_id_type=MESH)
        return carry

    lax.fori_loop(1, W, greet, 0)
    def greet_sec(d, carry):
        pl.semaphore_signal(
            barrier, inc=1, device_id={"sec": lax.rem(s + d, SEC)}, device_id_type=MESH)
        return carry

    lax.fori_loop(1, SEC, greet_sec, 0)

    for copy in ints:
        copy.wait()
    chosen, ranks, owners, slots, count = [], [], [], [], jnp.int32(0)
    for k in range(NB):
        chosen.append(sel[0, k] != 0)
        owners.append(lax.div(tgt[0, k], NB))
        slots.append(lax.rem(tgt[0, k], NB))
        ranks.append(count)
        count = count + jnp.where(chosen[k], 1, 0)

    def block_of(i):
        found = jnp.int32(0)
        for k in range(NB):
            found = found + jnp.where(chosen[k] & (ranks[k] == i), k, 0)
        return found

    lane = lax.broadcasted_iota(jnp.int32, (1, 128), 1)
    message = jnp.zeros((1, 128), jnp.int32)
    for i in range(ITEMS):
        place = jnp.int32(-1)
        for k in range(NB):
            place = place + jnp.where(chosen[k] & (ranks[k] == i), tgt[0, k] + 1, 0)
        value = jnp.where(place >= 0, place * SUB + lane % SUB + 1, 0)
        message = jnp.where(lane // SUB == i, value, message)
    msend[...] = message
    mrecv[w] = message

    item_of, slot_of = [], []
    for t in range(SEC):
        item, slot = jnp.int32(0), jnp.int32(0)
        for k in range(NB):
            hit = chosen[k] & (owners[k] == t)
            item = item + jnp.where(hit, ranks[k], 0)
            slot = slot + jnp.where(hit, slots[k] + 1, 0)
        item_of.append(item)
        slot_of.append(slot)
        xmsend[t] = jnp.zeros((1, 128), jnp.int32) + slot
    xmrecv[s] = xmsend[s]

    def send_message(d, carry):
        pltpu.make_async_remote_copy(
            msend, mrecv.at[w], mesh_sems.at[0], mesh_sems.at[1],
            device_id={"term": z_peer(d)}, device_id_type=MESH).start()
        return carry


    def send_slot(d, carry):
        peer = lax.rem(s + d, SEC)
        pltpu.make_async_remote_copy(
            xmsend.at[peer], xmrecv.at[s], xs_sem.at[0], xr_sem.at[0],
            device_id={"sec": peer}, device_id_type=MESH).start()
        return carry


    def wait_for(ref, sem):
        pltpu.make_async_copy(ref, ref, sem).wait()

    for copy in loads[:5]:
        copy.wait()
    for copy in loads[5:]:
        copy.start()

    row_id = lax.broadcasted_iota(jnp.int32, (BS, BS), 0)
    col_id = lax.broadcasted_iota(jnp.int32, (BS, BS), 1)

    def first_columns(i):
        k = block_of(i)
        block = psi_v[k]
        keep = (row_id < dims[0, k]) & (col_id < dims[1, k])
        block = jnp.where(keep, block, jnp.zeros_like(block))
        half_product = jnp.dot(
            left_v[k].reshape(2 * BS, BS), block, preferred_element_type=jnp.float32
        ).astype(jnp.bfloat16)
        half_product = jnp.concatenate([half_product[:BS], half_product[BS:]], axis=1)
        halves[i] = half_product
        total = jnp.dot(
            half_product, right_v[k].reshape(2 * BS, COLS), preferred_element_type=jnp.float32)
        return total.reshape(W * G, SUB, COLS)

    def other_columns(i):
        k = block_of(i)
        total = jnp.dot(
            halves[i], rest_v[k].reshape(2 * BS, BS - COLS), preferred_element_type=jnp.float32)
        last = total.reshape(W, G, SUB, BS - COLS)[:, G - XG:, :, BS - 2 * COLS:]
        xitems[i] = last.reshape(W * XG // 2, 2 * SUB, COLS).astype(jnp.bfloat16)
        return total.reshape(W * G, SUB, BS - COLS)

    def rows_of(p):
        return pl.ds(pl.multiple_of(p * 2 * SUB, 2 * SUB), 2 * SUB)

    def first_pair(p):
        both = [first_columns(2 * p), first_columns(2 * p + 1)]
        both = jnp.concatenate(both, axis=1).astype(jnp.bfloat16).reshape(W, G, 2 * SUB, COLS)
        for c in range(G):
            zsend[c, :, rows_of(p), :] = both[:, c]

    def other_pair(p, carry):
        both = [other_columns(2 * p), other_columns(2 * p + 1)]
        both = jnp.concatenate(both, axis=1).astype(jnp.bfloat16)
        both = both.reshape(W, G, 2 * SUB, BS - COLS)
        for c in range(G, C):
            at = (c // G - 1) * COLS
            zsend[c, :, rows_of(p), :] = both[:, c % G, :, at:at + COLS]
        return carry

    def send_pair(p):
        part = rows_of(p)

        def one(d, carry):
            peer = z_peer(d)
            pltpu.make_async_remote_copy(
                zsend.at[pl.ds(0, G), peer, part], zrecv.at[pl.ds(0, G), w, part],
                zs_sem.at[p], zr_sem.at[p],
                device_id={"term": peer}, device_id_type=MESH).start()
            return carry

        lax.fori_loop(1, W, one, 0)

    def next_pair(p, carry):
        first_pair(p)
        send_pair(p)
        return carry

    first_pair(0)
    pl.semaphore_wait(barrier, W - 1 + SEC - 1)
    send_pair(0)
    lax.fori_loop(1, W, send_message, 0)
    lax.fori_loop(1, SEC, send_slot, 0)
    lax.fori_loop(1, pairs, next_pair, 0)
    for copy in loads[5:]:
        copy.wait()
    lax.fori_loop(0, pairs, other_pair, 0)

    def send_chunk(c, carry):
        for dz, dc in z_turns:
            peer = lax.rem(z + dz, W // 2) * 2 + lax.rem(core + dc, 2)
            pltpu.make_async_remote_copy(
                zsend.at[c, peer], zrecv.at[c, w], zs_sem.at[pairs + c], zr_sem.at[pairs + c],
                device_id={"term": peer}, device_id_type=MESH).start()
        return carry


    for t in range(SEC):
        xsend[t] = jnp.where(slot_of[t] > 0, xitems[item_of[t]], jnp.zeros(xsend.shape[1:], jnp.bfloat16))

    for dy, dx in turns:
        peer = sec_at(lax.rem(y + dy, NY), lax.rem(x + dx, NX))
        pltpu.make_async_remote_copy(
            xsend.at[peer], xrecv.at[:, s], xs_sem.at[1], xr_sem.at[1],
            device_id={"sec": peer}, device_id_type=MESH).start()
    lax.fori_loop(G, C, send_chunk, 0)
    xrecv[:, s] = xsend[s]
    for c in range(C):
        zrecv[c, w] = zsend[c, w]

    wait_for(xmrecv.at[pl.ds(0, SEC - 1)], xr_sem.at[0])
    wide = -(-SEC * 2 * SUB // 128)
    lane = lax.broadcasted_iota(jnp.int32, (1, wide * 128), 1)
    slot = jnp.zeros((1, wide * 128), jnp.int32)
    for n in range(SEC):
        slot = jnp.where(lane // (2 * SUB) == n, jnp.concatenate([xmrecv[n]] * wide, axis=1), slot)
    place = (slot - 1) * SUB + lane % (2 * SUB) // SUB * (NB * SUB) + lane % SUB
    place = jnp.where(slot > 0, place, -1)[:, :SEC * 2 * SUB]
    row = lax.broadcasted_iota(jnp.int32, xhot.shape, 0)
    xhot[...] = jnp.where(row == place, 1.0, 0.0).astype(jnp.bfloat16)

    wait_for(mrecv.at[pl.ds(0, W - 1)], mesh_sems.at[1])
    width = -(-K // 128) * 128
    places = jnp.zeros((2 * SUB, width), jnp.int32)
    for n in range(W):
        wide = jnp.broadcast_to(mrecv[n], (2 * SUB, 128))
        if width > 128:
            wide = jnp.concatenate([wide, jnp.zeros((2 * SUB, width - 128), jnp.int32)], axis=1)
        places = places + (pltpu.roll(wide, n * R6, 1) if n else wide)
    places = places[:, :K]
    step = lax.broadcasted_iota(jnp.int32, (2 * SUB, K), 0) + 1

    def fill(b, carry):
        first = pl.multiple_of(b * 2 * SUB, 2 * SUB)
        onehot[pl.ds(first, 2 * SUB), :] = jnp.where(
            places == step + first, 1.0, 0.0).astype(jnp.bfloat16)
        return carry

    lax.fori_loop(0, NY * NX * NB * SUB // (2 * SUB), fill, 0)

    block_rows = NX * NB * SUB

    def by_target(c):
        @pl.when(c == 0)
        def _():
            for p in range(pairs):
                part = pl.ds(p * 2 * SUB, 2 * SUB)
                wait_for(zrecv.at[pl.ds(0, G), pl.ds(0, W - 1), part], zr_sem.at[p])

        @pl.when(c >= G)
        def _():
            wait_for(zrecv.at[c, pl.ds(0, W - 1)], zr_sem.at[pairs + c])

        arrived = zrecv[c].reshape(K, COLS)
        for yy in range(NY):
            part = jnp.dot(
                onehot[yy * block_rows:(yy + 1) * block_rows, :], arrived,
                preferred_element_type=jnp.float32)
            ybuf[c, yy] = part.astype(jnp.bfloat16).reshape(NX, NB * SUB, COLS)
        for d in range(1, NY):
            yy = lax.rem(y + d, NY)
            pltpu.make_async_remote_copy(
                ybuf.at[c, yy, :, pl.ds(0, half)], a1.at[c, d - 1], s1_sem.at[0, c], r1_sem.at[0, c],
                device_id={"sec": sec_at(yy, x)}, device_id_type=MESH).start()
        for d in range(1, NX):
            xx = lax.rem(x + d, NX)
            pltpu.make_async_remote_copy(
                ybuf.at[c, :, xx, pl.ds(half, half)], b1.at[c, d - 1], s1_sem.at[1, c], r1_sem.at[1, c],
                device_id={"sec": sec_at(y, xx)}, device_id_type=MESH).start()

    def by_target_at_once(c):
        wait_for(zrecv.at[c, pl.ds(0, W - 1)], zr_sem.at[pairs + c])
        arrived = zrecv[c].reshape(K, COLS)
        for dy in sorted(range(NY), key=lambda d: far(d, NY)):
            yy = lax.rem(y + dy, NY)
            first = pl.multiple_of(yy * block_rows, block_rows)
            part = jnp.dot(
                onehot[pl.ds(first, block_rows), :], arrived, preferred_element_type=jnp.float32)
            ybuf[c, yy] = part.astype(jnp.bfloat16).reshape(NX, NB * SUB, COLS)
            for dx in sorted(range(NX), key=lambda d: far(d, NX)):
                if dx or dy:
                    xx = lax.rem(x + dx, NX)
                    pltpu.make_async_remote_copy(
                        ybuf.at[c, yy, xx], direct.at[dy * NX + dx - 1], d_sem.at[0], d_sem.at[1],
                        device_id={"sec": sec_at(yy, xx)}, device_id_type=MESH).start()

    def add_direct(c):
        wait_for(direct, d_sem.at[1])
        total = ybuf[c, y, x].astype(jnp.float32)
        for n in range(SEC - 1):
            total = total + direct[n].astype(jnp.float32)
        fin[c] = total

    def one_axis(c):
        wait_for(a1.at[c], r1_sem.at[0, c])
        total = ybuf[c, y, :, :half, :].astype(jnp.float32)
        for n in range(NY - 1):
            total = total + a1[c, n].astype(jnp.float32)
        a2s[c] = total.astype(jnp.bfloat16)
        for d in range(1, NX):
            xx = lax.rem(x + d, NX)
            pltpu.make_async_remote_copy(
                a2s.at[c, xx], a2.at[c, d - 1], s2_sem.at[0, c], r2_sem.at[0, c],
                device_id={"sec": sec_at(y, xx)}, device_id_type=MESH).start()
        wait_for(b1.at[c], r1_sem.at[1, c])
        total = ybuf[c, :, x, half:, :].astype(jnp.float32)
        for n in range(NX - 1):
            total = total + b1[c, n].astype(jnp.float32)
        b2s[c] = total.astype(jnp.bfloat16)
        for d in range(1, NY):
            yy = lax.rem(y + d, NY)
            pltpu.make_async_remote_copy(
                b2s.at[c, yy], b2.at[c, d - 1], s2_sem.at[1, c], r2_sem.at[1, c],
                device_id={"sec": sec_at(yy, x)}, device_id_type=MESH).start()

    def other_axis(c):
        wait_for(a2.at[c], r2_sem.at[0, c])
        wait_for(b2.at[c], r2_sem.at[1, c])
        for own, others, place, at in ((a2s, a2, x, 0), (b2s, b2, y, half)):
            total = own[c, place].astype(jnp.float32)
            for n in range(others.shape[1]):
                total = total + others[c, n].astype(jnp.float32)
            fin[c, at:at + half, :] = total

    def place_items():
        wait_for(xrecv.at[:, pl.ds(0, SEC - 1)], xr_sem.at[1])
        for n in range(W * XG // 2):
            part = jnp.dot(
                xhot[...], xrecv[n].reshape(SEC * 2 * SUB, COLS), preferred_element_type=jnp.float32
            ).astype(jnp.bfloat16)
            for e in range(2):
                at = 2 * n + e
                to, first = at // XG, at % XG * NB * SUB
                xplaced[to % 2, to // 2, first:first + NB * SUB, :] = part[e * NB * SUB:(e + 1) * NB * SUB]
        pltpu.make_async_remote_copy(
            xplaced.at[1 - core], xcore, xs_sem.at[2], xr_sem.at[2],
            device_id={"term": w + 1 - 2 * core}, device_id_type=MESH).start()

    def add_cores():
        wait_for(xcore, xr_sem.at[2])
        xsum[...] = (xplaced[core].astype(jnp.float32) + xcore[...].astype(jnp.float32)).astype(jnp.bfloat16)
        for d in range(1, W // 2):
            peer = lax.rem(z + d, W // 2)
            pltpu.make_async_remote_copy(
                xsum.at[peer], xlast.at[d - 1], xs_sem.at[3], xr_sem.at[3],
                device_id={"term": peer * 2 + core}, device_id_type=MESH).start()

    def step_of(t, carry):
        @pl.when(t == G)
        def _():
            place_items()

        @pl.when(t == G + 1)
        def _():
            add_cores()

        @pl.when(t < C - 1)
        def _():
            by_target(t)

        @pl.when(t == C - 1)
        def _():
            by_target_at_once(C - 1)

        @pl.when((t >= 1) & (t < C))
        def _():
            one_axis(t - 1)

        @pl.when(t >= 2)
        def _():
            other_axis(t - 2)

        return carry

    lax.fori_loop(0, C + 1, step_of, 0)
    add_direct(C - 1)

    wait_for(xlast, xr_sem.at[3])
    total = xsum[z].astype(jnp.float32)
    for n in range(W // 2 - 1):
        total = total + xlast[n].astype(jnp.float32)
    fin[C:] = total.reshape(XG, NB * SUB, COLS)

    row_id = lax.broadcasted_iota(jnp.int32, (rows, BS), 0) + w * rows
    col_id = lax.broadcasted_iota(jnp.int32, (rows, BS), 1)
    for j in range(NB):
        keep = (row_id < dims[0, j]) & (col_id < dims[1, j])
        total = jnp.concatenate([
            jnp.concatenate([
                fin[q * G + g, j * SUB:(j + 1) * SUB, :] for q in range(BS // COLS)], axis=1)
            for g in range(G)], axis=0)
        out[j] = jnp.where(keep, total, 0.0).astype(out.dtype)

    wait_for(mrecv.at[pl.ds(0, W - 1)], mesh_sems.at[0])
    for p in range(pairs):
        part = pl.ds(p * 2 * SUB, 2 * SUB)
        wait_for(zsend.at[pl.ds(0, G), pl.ds(0, W - 1), part], zs_sem.at[p])

    def sent(c, carry):
        @pl.when(c >= G)
        def _():
            wait_for(zsend.at[c, pl.ds(0, W - 1)], zs_sem.at[pairs + c])

        @pl.when(c < C - 1)
        def _():
            wait_for(a1.at[c], s1_sem.at[0, c])
            wait_for(b1.at[c], s1_sem.at[1, c])
            wait_for(a2.at[c], s2_sem.at[0, c])
            wait_for(b2.at[c], s2_sem.at[1, c])

        return carry

    lax.fori_loop(0, C, sent, 0)
    wait_for(direct, d_sem.at[0])
    wait_for(xmrecv.at[pl.ds(0, SEC - 1)], xs_sem.at[0])
    wait_for(xsend.at[pl.ds(0, SEC - 1)], xs_sem.at[1])
    wait_for(xcore, xs_sem.at[2])
    wait_for(xlast, xs_sem.at[3])


def shards(W, SEC, psi, left_env, right_env, targets, selected, block_dims):
    NB, BS, _ = psi.shape
    NX = math.isqrt(SEC)
    NY = SEC // NX
    rows = BS // W
    C = BS // COLS * (rows // SUB) - XG
    pairs_here = W * XG // 2
    R6 = ITEMS * SUB
    half = NB * SUB // 2
    bf16, f32, i32 = jnp.bfloat16, jnp.float32, jnp.int32
    dma = pltpu.SemaphoreType.DMA
    hbm = pl.BlockSpec(memory_space=pltpu.HBM)
    return pl.pallas_call(
        functools.partial(kernel, W, NY, NX),
        out_shape=pltpu.VMEM((NB, rows, BS), bf16),
        in_specs=[hbm] * 6,
        out_specs=pl.BlockSpec(memory_space=pltpu.VMEM),
        scratch_shapes=[
            pltpu.SMEM((1, NB), i32),
            pltpu.SMEM((1, NB), i32),
            pltpu.SMEM((2, NB), i32),
            pltpu.VMEM((NB, BS, BS), bf16),
            pltpu.VMEM((NB, 2, BS, BS), bf16),
            pltpu.VMEM((NB, 2, BS, COLS), bf16),
            pltpu.VMEM((NB, 2, BS, BS - COLS), bf16),
            pltpu.VMEM((ITEMS, BS, 2 * BS), bf16),
            pltpu.VMEM((C, W, R6, COLS), bf16),
            pltpu.VMEM((C, W, R6, COLS), bf16),
            pltpu.VMEM((1, 128), i32),
            pltpu.VMEM((W, 1, 128), i32),
            pltpu.VMEM((SEC * NB * SUB, W * R6), bf16),
            pltpu.VMEM((C, NY, NX, NB * SUB, COLS), bf16),
            pltpu.VMEM((C - 1, NY - 1, NX, half, COLS), bf16),
            pltpu.VMEM((C - 1, NX - 1, NY, half, COLS), bf16),
            pltpu.VMEM((C - 1, NX, half, COLS), bf16),
            pltpu.VMEM((C - 1, NY, half, COLS), bf16),
            pltpu.VMEM((C - 1, NX - 1, half, COLS), bf16),
            pltpu.VMEM((C - 1, NY - 1, half, COLS), bf16),
            pltpu.VMEM((C + XG, NB * SUB, COLS), f32),
            pltpu.VMEM((SEC - 1, NB * SUB, COLS), bf16),
            pltpu.VMEM((SEC, 1, 128), i32),
            pltpu.VMEM((SEC, 1, 128), i32),
            pltpu.VMEM((ITEMS, pairs_here, 2 * SUB, COLS), bf16),
            pltpu.VMEM((SEC, pairs_here, 2 * SUB, COLS), bf16),
            pltpu.VMEM((pairs_here, SEC, 2 * SUB, COLS), bf16),
            pltpu.VMEM((2 * NB * SUB, SEC * 2 * SUB), bf16),
            pltpu.VMEM((2, W // 2, XG * NB * SUB, COLS), bf16),
            pltpu.VMEM((W // 2, XG * NB * SUB, COLS), bf16),
            pltpu.VMEM((W // 2, XG * NB * SUB, COLS), bf16),
            pltpu.VMEM((W // 2 - 1, XG * NB * SUB, COLS), bf16),
            dma((3,)), dma((7,)), dma((2,)), dma((ITEMS // 2 + C,)), dma((ITEMS // 2 + C,)),
            dma((2, C - 1)), dma((2, C - 1)), dma((2, C - 1)), dma((2, C - 1)), dma((4,)), dma((4,)), dma((2,)),
        ],
        compiler_params=pltpu.CompilerParams(
            collective_id=0, has_side_effects=True, vmem_limit_bytes=54 * 2**20),
        cost_estimate=pl.CostEstimate(flops=8 * 10**9, bytes_accessed=12 * 10**6, transcendentals=0),
        name="davidson",
    )(targets, selected, block_dims.T, psi, left_env, right_env)


def solution(mesh):
    W, SEC = mesh.shape["term"], mesh.shape["sec"]
    return jax.shard_map(
        functools.partial(shards, W, SEC),
        mesh=mesh,
        in_specs=(
            P("sec", None, None),
            P("term", None, "sec", None, None),
            P("term", None, "sec", None, None),
            P("term", "sec"),
            P("term", "sec"),
            P("sec", None),
        ),
        out_specs=P("sec", "term", None),
        check_vma=False,
    )
```

```python
import functools
import math

import jax
import jax.numpy as jnp
from jax import lax
from jax.experimental import pallas as pl
from jax.experimental.pallas import tpu as pltpu
from jax.sharding import PartitionSpec as P

MESH = pl.DeviceIdType.MESH
ITEMS = 6
COLS = 128
SUB = 8
XG = 2


def kernel(
    W, NY, NX,
    tgt_h, sel_h, dims_h, psi_h, left_h, right_h, out,
    tgt, sel, dims, psi_v, left_v, right_v, rest_v, halves, zsend, zrecv, msend, mrecv, onehot, ybuf,
    a1, b1, a2s, b2s, a2, b2, fin,
    direct, xmsend, xmrecv, xitems, xsend, xrecv, xhot, xplaced, xcore, xsum, xlast,
    int_sem, load_sem, mesh_sems, zs_sem, zr_sem, s1_sem, r1_sem, s2_sem, r2_sem, xs_sem, xr_sem, d_sem,
):
    w = lax.axis_index("term")
    s = lax.axis_index("sec")
    y, x = s // NX, s % NX
    NB, BS = psi_v.shape[0], psi_v.shape[1]
    rows = BS // W
    G = rows // SUB
    C = BS // COLS * G - XG
    R6 = ITEMS * SUB
    half = NB * SUB // 2
    pairs = ITEMS // 2
    K = W * R6
    SEC = NY * NX
    z, core = w // 2, w % 2

    ints = [(tgt_h, tgt), (sel_h, sel), (dims_h, dims)]
    ints = [pltpu.make_async_copy(a, b, int_sem.at[n]) for n, (a, b) in enumerate(ints)]
    for copy in ints:
        copy.start()
    loads = [(psi_h, psi_v)]
    for m in range(2):
        loads.append((left_h.at[0, m], left_v.at[:, m]))
    for m in range(2):
        loads.append((right_h.at[0, m, :, :, pl.ds(0, COLS)], right_v.at[:, m]))
    for m in range(2):
        loads.append((right_h.at[0, m, :, :, pl.ds(COLS, BS - COLS)], rest_v.at[:, m]))
    loads = [pltpu.make_async_copy(a, b, load_sem.at[n]) for n, (a, b) in enumerate(loads)]
    for copy in loads[:5]:
        copy.start()

    def z_peer(d):
        return lax.rem(w + d, W)

    def far(d, n):
        return -min(d, n - d)

    z_turns = sorted(((d, c) for d in range(1, W // 2) for c in range(2)), key=lambda t: far(t[0], W // 2))
    z_turns = [(0, 1)] + z_turns
    turns = [(dy, dx) for dy in range(NY) for dx in range(NX) if dy or dx]
    turns = sorted(turns, key=lambda t: far(t[0], NY) + far(t[1], NX))

    def sec_at(yy, xx):
        return yy * NX + xx

    barrier = pltpu.get_barrier_semaphore()

    def greet(d, carry):
        pl.semaphore_signal(barrier, inc=1, device_id={"term": z_peer(d)}, device_id_type=MESH)
        return carry

    lax.fori_loop(1, W, greet, 0)
    def greet_sec(d, carry):
        pl.semaphore_signal(
            barrier, inc=1, device_id={"sec": lax.rem(s + d, SEC)}, device_id_type=MESH)
        return carry

    lax.fori_loop(1, SEC, greet_sec, 0)

    for copy in ints:
        copy.wait()
    chosen, ranks, owners, slots, count = [], [], [], [], jnp.int32(0)
    for k in range(NB):
        chosen.append(sel[0, k] != 0)
        owners.append(lax.div(tgt[0, k], NB))
        slots.append(lax.rem(tgt[0, k], NB))
        ranks.append(count)
        count = count + jnp.where(chosen[k], 1, 0)

    def block_of(i):
        found = jnp.int32(0)
        for k in range(NB):
            found = found + jnp.where(chosen[k] & (ranks[k] == i), k, 0)
        return found

    lane = lax.broadcasted_iota(jnp.int32, (1, 128), 1)
    message = jnp.zeros((1, 128), jnp.int32)
    for i in range(ITEMS):
        place = jnp.int32(-1)
        for k in range(NB):
            place = place + jnp.where(chosen[k] & (ranks[k] == i), tgt[0, k] + 1, 0)
        value = jnp.where(place >= 0, place * SUB + lane % SUB + 1, 0)
        message = jnp.where(lane // SUB == i, value, message)
    msend[...] = message
    mrecv[w] = message

    item_of, slot_of = [], []
    for t in range(SEC):
        item, slot = jnp.int32(0), jnp.int32(0)
        for k in range(NB):
            hit = chosen[k] & (owners[k] == t)
            item = item + jnp.where(hit, ranks[k], 0)
            slot = slot + jnp.where(hit, slots[k] + 1, 0)
        item_of.append(item)
        slot_of.append(slot)
        xmsend[t] = jnp.zeros((1, 128), jnp.int32) + slot
    xmrecv[s] = xmsend[s]

    def send_message(d, carry):
        pltpu.make_async_remote_copy(
            msend, mrecv.at[w], mesh_sems.at[0], mesh_sems.at[1],
            device_id={"term": z_peer(d)}, device_id_type=MESH).start()
        return carry


    def send_slot(d, carry):
        peer = lax.rem(s + d, SEC)
        pltpu.make_async_remote_copy(
            xmsend.at[peer], xmrecv.at[s], xs_sem.at[0], xr_sem.at[0],
            device_id={"sec": peer}, device_id_type=MESH).start()
        return carry


    def wait_for(ref, sem):
        pltpu.make_async_copy(ref, ref, sem).wait()

    for copy in loads[:5]:
        copy.wait()
    for copy in loads[5:]:
        copy.start()

    row_id = lax.broadcasted_iota(jnp.int32, (BS, BS), 0)
    col_id = lax.broadcasted_iota(jnp.int32, (BS, BS), 1)

    def first_columns(i):
        k = block_of(i)
        block = psi_v[k]
        keep = (row_id < dims[0, k]) & (col_id < dims[1, k])
        block = jnp.where(keep, block, jnp.zeros_like(block))
        half_product = jnp.dot(
            left_v[k].reshape(2 * BS, BS), block, preferred_element_type=jnp.float32
        ).astype(jnp.bfloat16)
        half_product = jnp.concatenate([half_product[:BS], half_product[BS:]], axis=1)
        halves[i] = half_product
        total = jnp.dot(
            half_product, right_v[k].reshape(2 * BS, COLS), preferred_element_type=jnp.float32)
        return total.reshape(W * G, SUB, COLS)

    def other_columns(i, first, width):
        side = rest_v[block_of(i), :, :, first - COLS:first - COLS + width].reshape(2 * BS, width)
        total = jnp.dot(halves[i], side, preferred_element_type=jnp.float32)
        return total.reshape(W * G, SUB, width)

    def rows_of(p):
        return pl.ds(pl.multiple_of(p * 2 * SUB, 2 * SUB), 2 * SUB)

    def first_pair(p):
        both = [first_columns(2 * p), first_columns(2 * p + 1)]
        both = jnp.concatenate(both, axis=1).astype(jnp.bfloat16).reshape(W, G, 2 * SUB, COLS)
        for c in range(G):
            zsend[c, :, rows_of(p), :] = both[:, c]

    def put(p, both, first, width):
        both = jnp.concatenate(both, axis=1).astype(jnp.bfloat16).reshape(W, G, 2 * SUB, width)
        for c in range(first // COLS * G, min(C, (first + width) // COLS * G)):
            at = c // G * COLS - first
            zsend[c, :, rows_of(p), :] = both[:, c % G, :, at:at + COLS]

    def last_pair(p, carry):
        both = []
        for e in range(2):
            total = other_columns(2 * p + e, BS - COLS, COLS)
            both.append(total)
            last = total.reshape(W, G, SUB, COLS)[:, G - XG:]
            xitems[2 * p + e] = last.reshape(W * XG // 2, 2 * SUB, COLS).astype(jnp.bfloat16)
        put(p, both, BS - COLS, COLS)
        return carry

    def middle_pair(p, carry):
        width = BS - 2 * COLS
        put(p, [other_columns(2 * p + e, COLS, width) for e in range(2)], COLS, width)
        return carry

    def send_pair(p):
        part = rows_of(p)

        def one(d, carry):
            peer = z_peer(d)
            pltpu.make_async_remote_copy(
                zsend.at[pl.ds(0, G), peer, part], zrecv.at[pl.ds(0, G), w, part],
                zs_sem.at[p], zr_sem.at[p],
                device_id={"term": peer}, device_id_type=MESH).start()
            return carry

        lax.fori_loop(1, W, one, 0)

    def next_pair(p, carry):
        first_pair(p)
        send_pair(p)
        return carry

    first_pair(0)
    pl.semaphore_wait(barrier, W - 1 + SEC - 1)
    send_pair(0)
    lax.fori_loop(1, W, send_message, 0)
    lax.fori_loop(1, SEC, send_slot, 0)
    lax.fori_loop(1, pairs, next_pair, 0)
    for copy in loads[5:]:
        copy.wait()
    lax.fori_loop(0, pairs, last_pair, 0)

    def send_chunk(c, carry):
        for dz, dc in z_turns:
            peer = lax.rem(z + dz, W // 2) * 2 + lax.rem(core + dc, 2)
            pltpu.make_async_remote_copy(
                zsend.at[c, peer], zrecv.at[c, w], zs_sem.at[pairs + c], zr_sem.at[pairs + c],
                device_id={"term": peer}, device_id_type=MESH).start()
        return carry


    for t in range(SEC):
        xsend[t] = jnp.where(slot_of[t] > 0, xitems[item_of[t]], jnp.zeros(xsend.shape[1:], jnp.bfloat16))

    for dy, dx in turns:
        peer = sec_at(lax.rem(y + dy, NY), lax.rem(x + dx, NX))
        pltpu.make_async_remote_copy(
            xsend.at[peer], xrecv.at[:, s], xs_sem.at[1], xr_sem.at[1],
            device_id={"sec": peer}, device_id_type=MESH).start()
    if BS > 2 * COLS:
        lax.fori_loop(0, pairs, middle_pair, 0)
    lax.fori_loop(G, C, send_chunk, 0)
    xrecv[:, s] = xsend[s]
    for c in range(C):
        zrecv[c, w] = zsend[c, w]

    wait_for(xmrecv.at[pl.ds(0, SEC - 1)], xr_sem.at[0])
    wide = -(-SEC * 2 * SUB // 128)
    lane = lax.broadcasted_iota(jnp.int32, (1, wide * 128), 1)
    slot = jnp.zeros((1, wide * 128), jnp.int32)
    for n in range(SEC):
        slot = jnp.where(lane // (2 * SUB) == n, jnp.concatenate([xmrecv[n]] * wide, axis=1), slot)
    place = (slot - 1) * SUB + lane % (2 * SUB) // SUB * (NB * SUB) + lane % SUB
    place = jnp.where(slot > 0, place, -1)[:, :SEC * 2 * SUB]
    row = lax.broadcasted_iota(jnp.int32, xhot.shape, 0)
    xhot[...] = jnp.where(row == place, 1.0, 0.0).astype(jnp.bfloat16)

    wait_for(mrecv.at[pl.ds(0, W - 1)], mesh_sems.at[1])
    width = -(-K // 128) * 128
    places = jnp.zeros((2 * SUB, width), jnp.int32)
    for n in range(W):
        wide = jnp.broadcast_to(mrecv[n], (2 * SUB, 128))
        if width > 128:
            wide = jnp.concatenate([wide, jnp.zeros((2 * SUB, width - 128), jnp.int32)], axis=1)
        places = places + (pltpu.roll(wide, n * R6, 1) if n else wide)
    places = places[:, :K]
    step = lax.broadcasted_iota(jnp.int32, (2 * SUB, K), 0) + 1

    def fill(b, carry):
        first = pl.multiple_of(b * 2 * SUB, 2 * SUB)
        onehot[pl.ds(first, 2 * SUB), :] = jnp.where(
            places == step + first, 1.0, 0.0).astype(jnp.bfloat16)
        return carry

    lax.fori_loop(0, NY * NX * NB * SUB // (2 * SUB), fill, 0)

    block_rows = NX * NB * SUB

    def by_target(c):
        @pl.when(c == 0)
        def _():
            for p in range(pairs):
                part = pl.ds(p * 2 * SUB, 2 * SUB)
                wait_for(zrecv.at[pl.ds(0, G), pl.ds(0, W - 1), part], zr_sem.at[p])

        @pl.when(c >= G)
        def _():
            wait_for(zrecv.at[c, pl.ds(0, W - 1)], zr_sem.at[pairs + c])

        arrived = zrecv[c].reshape(K, COLS)
        for yy in range(NY):
            part = jnp.dot(
                onehot[yy * block_rows:(yy + 1) * block_rows, :], arrived,
                preferred_element_type=jnp.float32)
            ybuf[c, yy] = part.astype(jnp.bfloat16).reshape(NX, NB * SUB, COLS)
        for d in range(1, NY):
            yy = lax.rem(y + d, NY)
            pltpu.make_async_remote_copy(
                ybuf.at[c, yy, :, pl.ds(0, half)], a1.at[c, d - 1], s1_sem.at[0, c], r1_sem.at[0, c],
                device_id={"sec": sec_at(yy, x)}, device_id_type=MESH).start()
        for d in range(1, NX):
            xx = lax.rem(x + d, NX)
            pltpu.make_async_remote_copy(
                ybuf.at[c, :, xx, pl.ds(half, half)], b1.at[c, d - 1], s1_sem.at[1, c], r1_sem.at[1, c],
                device_id={"sec": sec_at(y, xx)}, device_id_type=MESH).start()

    def by_target_at_once(c):
        wait_for(zrecv.at[c, pl.ds(0, W - 1)], zr_sem.at[pairs + c])
        arrived = zrecv[c].reshape(K, COLS)
        for dy in sorted(range(NY), key=lambda d: far(d, NY)):
            yy = lax.rem(y + dy, NY)
            first = pl.multiple_of(yy * block_rows, block_rows)
            part = jnp.dot(
                onehot[pl.ds(first, block_rows), :], arrived, preferred_element_type=jnp.float32)
            ybuf[c, yy] = part.astype(jnp.bfloat16).reshape(NX, NB * SUB, COLS)
            for dx in sorted(range(NX), key=lambda d: far(d, NX)):
                if dx or dy:
                    xx = lax.rem(x + dx, NX)
                    pltpu.make_async_remote_copy(
                        ybuf.at[c, yy, xx], direct.at[dy * NX + dx - 1], d_sem.at[0], d_sem.at[1],
                        device_id={"sec": sec_at(yy, xx)}, device_id_type=MESH).start()

    def add_direct(c):
        wait_for(direct, d_sem.at[1])
        total = ybuf[c, y, x].astype(jnp.float32)
        for n in range(SEC - 1):
            total = total + direct[n].astype(jnp.float32)
        fin[c] = total

    def one_axis(c):
        wait_for(a1.at[c], r1_sem.at[0, c])
        total = ybuf[c, y, :, :half, :].astype(jnp.float32)
        for n in range(NY - 1):
            total = total + a1[c, n].astype(jnp.float32)
        a2s[c] = total.astype(jnp.bfloat16)
        for d in range(1, NX):
            xx = lax.rem(x + d, NX)
            pltpu.make_async_remote_copy(
                a2s.at[c, xx], a2.at[c, d - 1], s2_sem.at[0, c], r2_sem.at[0, c],
                device_id={"sec": sec_at(y, xx)}, device_id_type=MESH).start()
        wait_for(b1.at[c], r1_sem.at[1, c])
        total = ybuf[c, :, x, half:, :].astype(jnp.float32)
        for n in range(NX - 1):
            total = total + b1[c, n].astype(jnp.float32)
        b2s[c] = total.astype(jnp.bfloat16)
        for d in range(1, NY):
            yy = lax.rem(y + d, NY)
            pltpu.make_async_remote_copy(
                b2s.at[c, yy], b2.at[c, d - 1], s2_sem.at[1, c], r2_sem.at[1, c],
                device_id={"sec": sec_at(yy, x)}, device_id_type=MESH).start()

    def other_axis(c):
        wait_for(a2.at[c], r2_sem.at[0, c])
        wait_for(b2.at[c], r2_sem.at[1, c])
        for own, others, place, at in ((a2s, a2, x, 0), (b2s, b2, y, half)):
            total = own[c, place].astype(jnp.float32)
            for n in range(others.shape[1]):
                total = total + others[c, n].astype(jnp.float32)
            fin[c, at:at + half, :] = total

    def place_items():
        wait_for(xrecv.at[:, pl.ds(0, SEC - 1)], xr_sem.at[1])
        for n in range(W * XG // 2):
            part = jnp.dot(
                xhot[...], xrecv[n].reshape(SEC * 2 * SUB, COLS), preferred_element_type=jnp.float32
            ).astype(jnp.bfloat16)
            for e in range(2):
                at = 2 * n + e
                to, first = at // XG, at % XG * NB * SUB
                xplaced[to % 2, to // 2, first:first + NB * SUB, :] = part[e * NB * SUB:(e + 1) * NB * SUB]
        pltpu.make_async_remote_copy(
            xplaced.at[1 - core], xcore, xs_sem.at[2], xr_sem.at[2],
            device_id={"term": w + 1 - 2 * core}, device_id_type=MESH).start()

    def add_cores():
        wait_for(xcore, xr_sem.at[2])
        xsum[...] = (xplaced[core].astype(jnp.float32) + xcore[...].astype(jnp.float32)).astype(jnp.bfloat16)
        for d in range(1, W // 2):
            peer = lax.rem(z + d, W // 2)
            pltpu.make_async_remote_copy(
                xsum.at[peer], xlast.at[d - 1], xs_sem.at[3], xr_sem.at[3],
                device_id={"term": peer * 2 + core}, device_id_type=MESH).start()

    def step_of(t, carry):
        @pl.when(t == G)
        def _():
            place_items()

        @pl.when(t == G + 1)
        def _():
            add_cores()

        @pl.when(t < C - 1)
        def _():
            by_target(t)

        @pl.when(t == C - 1)
        def _():
            by_target_at_once(C - 1)

        @pl.when((t >= 1) & (t < C))
        def _():
            one_axis(t - 1)

        @pl.when(t >= 2)
        def _():
            other_axis(t - 2)

        return carry

    lax.fori_loop(0, C + 1, step_of, 0)
    add_direct(C - 1)

    wait_for(xlast, xr_sem.at[3])
    total = xsum[z].astype(jnp.float32)
    for n in range(W // 2 - 1):
        total = total + xlast[n].astype(jnp.float32)
    fin[C:] = total.reshape(XG, NB * SUB, COLS)

    row_id = lax.broadcasted_iota(jnp.int32, (rows, BS), 0) + w * rows
    col_id = lax.broadcasted_iota(jnp.int32, (rows, BS), 1)
    for j in range(NB):
        keep = (row_id < dims[0, j]) & (col_id < dims[1, j])
        total = jnp.concatenate([
            jnp.concatenate([
                fin[q * G + g, j * SUB:(j + 1) * SUB, :] for q in range(BS // COLS)], axis=1)
            for g in range(G)], axis=0)
        out[j] = jnp.where(keep, total, 0.0).astype(out.dtype)

    wait_for(mrecv.at[pl.ds(0, W - 1)], mesh_sems.at[0])
    for p in range(pairs):
        part = pl.ds(p * 2 * SUB, 2 * SUB)
        wait_for(zsend.at[pl.ds(0, G), pl.ds(0, W - 1), part], zs_sem.at[p])

    def sent(c, carry):
        @pl.when(c >= G)
        def _():
            wait_for(zsend.at[c, pl.ds(0, W - 1)], zs_sem.at[pairs + c])

        @pl.when(c < C - 1)
        def _():
            wait_for(a1.at[c], s1_sem.at[0, c])
            wait_for(b1.at[c], s1_sem.at[1, c])
            wait_for(a2.at[c], s2_sem.at[0, c])
            wait_for(b2.at[c], s2_sem.at[1, c])

        return carry

    lax.fori_loop(0, C, sent, 0)
    wait_for(direct, d_sem.at[0])
    wait_for(xmrecv.at[pl.ds(0, SEC - 1)], xs_sem.at[0])
    wait_for(xsend.at[pl.ds(0, SEC - 1)], xs_sem.at[1])
    wait_for(xcore, xs_sem.at[2])
    wait_for(xlast, xs_sem.at[3])


def shards(W, SEC, psi, left_env, right_env, targets, selected, block_dims):
    NB, BS, _ = psi.shape
    NX = math.isqrt(SEC)
    NY = SEC // NX
    rows = BS // W
    C = BS // COLS * (rows // SUB) - XG
    pairs_here = W * XG // 2
    R6 = ITEMS * SUB
    half = NB * SUB // 2
    bf16, f32, i32 = jnp.bfloat16, jnp.float32, jnp.int32
    dma = pltpu.SemaphoreType.DMA
    hbm = pl.BlockSpec(memory_space=pltpu.HBM)
    return pl.pallas_call(
        functools.partial(kernel, W, NY, NX),
        out_shape=pltpu.VMEM((NB, rows, BS), bf16),
        in_specs=[hbm] * 6,
        out_specs=pl.BlockSpec(memory_space=pltpu.VMEM),
        scratch_shapes=[
            pltpu.SMEM((1, NB), i32),
            pltpu.SMEM((1, NB), i32),
            pltpu.SMEM((2, NB), i32),
            pltpu.VMEM((NB, BS, BS), bf16),
            pltpu.VMEM((NB, 2, BS, BS), bf16),
            pltpu.VMEM((NB, 2, BS, COLS), bf16),
            pltpu.VMEM((NB, 2, BS, BS - COLS), bf16),
            pltpu.VMEM((ITEMS, BS, 2 * BS), bf16),
            pltpu.VMEM((C, W, R6, COLS), bf16),
            pltpu.VMEM((C, W, R6, COLS), bf16),
            pltpu.VMEM((1, 128), i32),
            pltpu.VMEM((W, 1, 128), i32),
            pltpu.VMEM((SEC * NB * SUB, W * R6), bf16),
            pltpu.VMEM((C, NY, NX, NB * SUB, COLS), bf16),
            pltpu.VMEM((C - 1, NY - 1, NX, half, COLS), bf16),
            pltpu.VMEM((C - 1, NX - 1, NY, half, COLS), bf16),
            pltpu.VMEM((C - 1, NX, half, COLS), bf16),
            pltpu.VMEM((C - 1, NY, half, COLS), bf16),
            pltpu.VMEM((C - 1, NX - 1, half, COLS), bf16),
            pltpu.VMEM((C - 1, NY - 1, half, COLS), bf16),
            pltpu.VMEM((C + XG, NB * SUB, COLS), f32),
            pltpu.VMEM((SEC - 1, NB * SUB, COLS), bf16),
            pltpu.VMEM((SEC, 1, 128), i32),
            pltpu.VMEM((SEC, 1, 128), i32),
            pltpu.VMEM((ITEMS, pairs_here, 2 * SUB, COLS), bf16),
            pltpu.VMEM((SEC, pairs_here, 2 * SUB, COLS), bf16),
            pltpu.VMEM((pairs_here, SEC, 2 * SUB, COLS), bf16),
            pltpu.VMEM((2 * NB * SUB, SEC * 2 * SUB), bf16),
            pltpu.VMEM((2, W // 2, XG * NB * SUB, COLS), bf16),
            pltpu.VMEM((W // 2, XG * NB * SUB, COLS), bf16),
            pltpu.VMEM((W // 2, XG * NB * SUB, COLS), bf16),
            pltpu.VMEM((W // 2 - 1, XG * NB * SUB, COLS), bf16),
            dma((3,)), dma((7,)), dma((2,)), dma((ITEMS // 2 + C,)), dma((ITEMS // 2 + C,)),
            dma((2, C - 1)), dma((2, C - 1)), dma((2, C - 1)), dma((2, C - 1)), dma((4,)), dma((4,)), dma((2,)),
        ],
        compiler_params=pltpu.CompilerParams(
            collective_id=0, has_side_effects=True, vmem_limit_bytes=54 * 2**20),
        cost_estimate=pl.CostEstimate(flops=8 * 10**9, bytes_accessed=12 * 10**6, transcendentals=0),
        name="davidson",
    )(targets, selected, block_dims.T, psi, left_env, right_env)


def solution(mesh):
    W, SEC = mesh.shape["term"], mesh.shape["sec"]
    return jax.shard_map(
        functools.partial(shards, W, SEC),
        mesh=mesh,
        in_specs=(
            P("sec", None, None),
            P("term", None, "sec", None, None),
            P("term", None, "sec", None, None),
            P("term", "sec"),
            P("term", "sec"),
            P("sec", None),
        ),
        out_specs=P("sec", "term", None),
        check_vma=False,
    )
```

```python
import functools
import math

import jax
import jax.numpy as jnp
from jax import lax
from jax.experimental import pallas as pl
from jax.experimental.pallas import tpu as pltpu
from jax.sharding import PartitionSpec as P

MESH = pl.DeviceIdType.MESH
ITEMS = 6
COLS = 128
SUB = 8
XG = 2


def kernel(
    W, NY, NX,
    tgt_h, sel_h, dims_h, psi_h, left_h, right_h, out,
    tgt, sel, dims, psi_v, left_v, right_v, rest_v, halves, zsend, zrecv, msend, mrecv, onehot, ybuf,
    a1, b1, a2s, b2s, a2, b2, fin,
    direct, xmsend, xmrecv, xitems, xsend, xrecv, xhot, xplaced, xcore, xsum, xlast,
    int_sem, load_sem, mesh_sems, zs_sem, zr_sem, s1_sem, r1_sem, s2_sem, r2_sem, xs_sem, xr_sem, d_sem,
):
    w = lax.axis_index("term")
    s = lax.axis_index("sec")
    y, x = s // NX, s % NX
    NB, BS = psi_v.shape[0], psi_v.shape[1]
    rows = BS // W
    G = rows // SUB
    C = BS // COLS * G - XG
    R6 = ITEMS * SUB
    half = NB * SUB // 2
    pairs = ITEMS // 2
    K = W * R6
    SEC = NY * NX
    z, core = w // 2, w % 2

    ints = [(tgt_h, tgt), (sel_h, sel), (dims_h, dims)]
    ints = [pltpu.make_async_copy(a, b, int_sem.at[n]) for n, (a, b) in enumerate(ints)]
    for copy in ints:
        copy.start()
    loads = [(psi_h, psi_v)]
    for m in range(2):
        loads.append((left_h.at[0, m], left_v.at[:, m]))
    for m in range(2):
        loads.append((right_h.at[0, m, :, :, pl.ds(0, COLS)], right_v.at[:, m]))
    for m in range(2):
        loads.append((right_h.at[0, m, :, :, pl.ds(COLS, BS - COLS)], rest_v.at[:, m]))
    loads = [pltpu.make_async_copy(a, b, load_sem.at[n]) for n, (a, b) in enumerate(loads)]
    for copy in loads[:5]:
        copy.start()

    def z_peer(d):
        return lax.rem(w + d, W)

    def far(d, n):
        return -min(d, n - d)

    z_turns = sorted(((d, c) for d in range(1, W // 2) for c in range(2)), key=lambda t: far(t[0], W // 2))
    z_turns = [(0, 1)] + z_turns
    turns = [(dy, dx) for dy in range(NY) for dx in range(NX) if dy or dx]
    turns = sorted(turns, key=lambda t: far(t[0], NY) + far(t[1], NX))

    def sec_at(yy, xx):
        return yy * NX + xx

    barrier = pltpu.get_barrier_semaphore()

    def greet(d, carry):
        pl.semaphore_signal(barrier, inc=1, device_id={"term": z_peer(d)}, device_id_type=MESH)
        return carry

    lax.fori_loop(1, W, greet, 0)
    def greet_sec(d, carry):
        pl.semaphore_signal(
            barrier, inc=1, device_id={"sec": lax.rem(s + d, SEC)}, device_id_type=MESH)
        return carry

    lax.fori_loop(1, SEC, greet_sec, 0)

    for copy in ints:
        copy.wait()
    chosen, ranks, owners, slots, count = [], [], [], [], jnp.int32(0)
    for k in range(NB):
        chosen.append(sel[0, k] != 0)
        owners.append(lax.div(tgt[0, k], NB))
        slots.append(lax.rem(tgt[0, k], NB))
        ranks.append(count)
        count = count + jnp.where(chosen[k], 1, 0)

    def block_of(i):
        found = jnp.int32(0)
        for k in range(NB):
            found = found + jnp.where(chosen[k] & (ranks[k] == i), k, 0)
        return found

    lane = lax.broadcasted_iota(jnp.int32, (1, 128), 1)
    message = jnp.zeros((1, 128), jnp.int32)
    for i in range(ITEMS):
        place = jnp.int32(-1)
        for k in range(NB):
            place = place + jnp.where(chosen[k] & (ranks[k] == i), tgt[0, k] + 1, 0)
        value = jnp.where(place >= 0, place * SUB + lane % SUB + 1, 0)
        message = jnp.where(lane // SUB == i, value, message)
    msend[...] = message
    mrecv[w] = message

    item_of, slot_of = [], []
    for t in range(SEC):
        item, slot = jnp.int32(0), jnp.int32(0)
        for k in range(NB):
            hit = chosen[k] & (owners[k] == t)
            item = item + jnp.where(hit, ranks[k], 0)
            slot = slot + jnp.where(hit, slots[k] + 1, 0)
        item_of.append(item)
        slot_of.append(slot)
        xmsend[t] = jnp.zeros((1, 128), jnp.int32) + slot
    xmrecv[s] = xmsend[s]

    def send_message(d, carry):
        pltpu.make_async_remote_copy(
            msend, mrecv.at[w], mesh_sems.at[0], mesh_sems.at[1],
            device_id={"term": z_peer(d)}, device_id_type=MESH).start()
        return carry


    def send_slot(d, carry):
        peer = lax.rem(s + d, SEC)
        pltpu.make_async_remote_copy(
            xmsend.at[peer], xmrecv.at[s], xs_sem.at[0], xr_sem.at[0],
            device_id={"sec": peer}, device_id_type=MESH).start()
        return carry


    def wait_for(ref, sem):
        pltpu.make_async_copy(ref, ref, sem).wait()

    for copy in loads[:5]:
        copy.wait()
    for copy in loads[5:]:
        copy.start()

    row_id = lax.broadcasted_iota(jnp.int32, (BS, BS), 0)
    col_id = lax.broadcasted_iota(jnp.int32, (BS, BS), 1)

    def first_columns(i):
        k = block_of(i)
        block = psi_v[k]
        keep = (row_id < dims[0, k]) & (col_id < dims[1, k])
        block = jnp.where(keep, block, jnp.zeros_like(block))
        half_product = jnp.dot(
            left_v[k].reshape(2 * BS, BS), block, preferred_element_type=jnp.float32
        ).astype(jnp.bfloat16)
        half_product = jnp.concatenate([half_product[:BS], half_product[BS:]], axis=1)
        halves[i] = half_product
        total = jnp.dot(
            half_product, right_v[k].reshape(2 * BS, COLS), preferred_element_type=jnp.float32)
        return total.reshape(W * G, SUB, COLS)

    def other_columns(i):
        k = block_of(i)
        total = jnp.dot(
            halves[i], rest_v[k].reshape(2 * BS, BS - COLS), preferred_element_type=jnp.float32)
        last = total.reshape(W, G, SUB, BS - COLS)[:, G - XG:, :, BS - 2 * COLS:]
        xitems[i] = last.reshape(W * XG // 2, 2 * SUB, COLS).astype(jnp.bfloat16)
        return total.reshape(W * G, SUB, BS - COLS)

    def rows_of(p):
        return pl.ds(pl.multiple_of(p * 2 * SUB, 2 * SUB), 2 * SUB)

    def first_pair(p):
        both = [first_columns(2 * p), first_columns(2 * p + 1)]
        both = jnp.concatenate(both, axis=1).astype(jnp.bfloat16).reshape(W, G, 2 * SUB, COLS)
        for c in range(G):
            zsend[c, :, rows_of(p), :] = both[:, c]

    def other_pair(p, carry):
        both = [other_columns(2 * p), other_columns(2 * p + 1)]
        both = jnp.concatenate(both, axis=1).astype(jnp.bfloat16)
        both = both.reshape(W, G, 2 * SUB, BS - COLS)
        for c in range(G, C):
            at = (c // G - 1) * COLS
            zsend[c, :, rows_of(p), :] = both[:, c % G, :, at:at + COLS]
        return carry

    def send_pair(p):
        part = rows_of(p)

        def one(d, carry):
            peer = z_peer(d)
            pltpu.make_async_remote_copy(
                zsend.at[pl.ds(0, G), peer, part], zrecv.at[pl.ds(0, G), w, part],
                zs_sem.at[p], zr_sem.at[p],
                device_id={"term": peer}, device_id_type=MESH).start()
            return carry

        lax.fori_loop(1, W, one, 0)

    def next_pair(p, carry):
        first_pair(p)
        send_pair(p)
        return carry

    first_pair(0)
    pl.semaphore_wait(barrier, W - 1 + SEC - 1)
    send_pair(0)
    lax.fori_loop(1, W, send_message, 0)
    lax.fori_loop(1, SEC, send_slot, 0)
    lax.fori_loop(1, pairs, next_pair, 0)
    for copy in loads[5:]:
        copy.wait()
    lax.fori_loop(0, pairs, other_pair, 0)

    def send_chunk(c, carry):
        for dz, dc in z_turns:
            peer = lax.rem(z + dz, W // 2) * 2 + lax.rem(core + dc, 2)
            pltpu.make_async_remote_copy(
                zsend.at[c, peer], zrecv.at[c, w], zs_sem.at[pairs + c], zr_sem.at[pairs + c],
                device_id={"term": peer}, device_id_type=MESH).start()
        return carry


    for t in range(SEC):
        xsend[t] = jnp.where(slot_of[t] > 0, xitems[item_of[t]], jnp.zeros(xsend.shape[1:], jnp.bfloat16))

    for dy, dx in turns:
        peer = sec_at(lax.rem(y + dy, NY), lax.rem(x + dx, NX))
        pltpu.make_async_remote_copy(
            xsend.at[peer], xrecv.at[:, s], xs_sem.at[1], xr_sem.at[1],
            device_id={"sec": peer}, device_id_type=MESH).start()
    lax.fori_loop(G, C, send_chunk, 0)
    xrecv[:, s] = xsend[s]
    for c in range(C):
        zrecv[c, w] = zsend[c, w]

    wait_for(xmrecv.at[pl.ds(0, SEC - 1)], xr_sem.at[0])
    wide = -(-SEC * 2 * SUB // 128)
    lane = lax.broadcasted_iota(jnp.int32, (1, wide * 128), 1)
    slot = jnp.zeros((1, wide * 128), jnp.int32)
    for n in range(SEC):
        slot = jnp.where(lane // (2 * SUB) == n, jnp.concatenate([xmrecv[n]] * wide, axis=1), slot)
    place = (slot - 1) * SUB + lane % (2 * SUB) // SUB * (NB * SUB) + lane % SUB
    place = jnp.where(slot > 0, place, -1)[:, :SEC * 2 * SUB]
    row = lax.broadcasted_iota(jnp.int32, xhot.shape, 0)
    xhot[...] = jnp.where(row == place, 1.0, 0.0).astype(jnp.bfloat16)

    wait_for(mrecv.at[pl.ds(0, W - 1)], mesh_sems.at[1])
    width = -(-K // 128) * 128
    places = jnp.zeros((2 * SUB, width), jnp.int32)
    for n in range(W):
        wide = jnp.broadcast_to(mrecv[n], (2 * SUB, 128))
        if width > 128:
            wide = jnp.concatenate([wide, jnp.zeros((2 * SUB, width - 128), jnp.int32)], axis=1)
        places = places + (pltpu.roll(wide, n * R6, 1) if n else wide)
    places = places[:, :K]
    step = lax.broadcasted_iota(jnp.int32, (2 * SUB, K), 0) + 1

    def fill(b, carry):
        first = pl.multiple_of(b * 2 * SUB, 2 * SUB)
        onehot[pl.ds(first, 2 * SUB), :] = jnp.where(
            places == step + first, 1.0, 0.0).astype(jnp.bfloat16)
        return carry

    lax.fori_loop(0, NY * NX * NB * SUB // (2 * SUB), fill, 0)

    block_rows = NX * NB * SUB

    def by_target(c):
        @pl.when(c == 0)
        def _():
            for p in range(pairs):
                part = pl.ds(p * 2 * SUB, 2 * SUB)
                wait_for(zrecv.at[pl.ds(0, G), pl.ds(0, W - 1), part], zr_sem.at[p])

        @pl.when(c >= G)
        def _():
            wait_for(zrecv.at[c, pl.ds(0, W - 1)], zr_sem.at[pairs + c])

        arrived = zrecv[c].reshape(K, COLS)
        for yy in range(NY):
            part = jnp.dot(
                onehot[yy * block_rows:(yy + 1) * block_rows, :], arrived,
                preferred_element_type=jnp.float32)
            ybuf[c, yy] = part.astype(jnp.bfloat16).reshape(NX, NB * SUB, COLS)
        for d in sorted(range(1, NY), key=lambda d: far(d, NY)):
            yy = lax.rem(y + d, NY)
            pltpu.make_async_remote_copy(
                ybuf.at[c, yy, :, pl.ds(0, half)], a1.at[c, d - 1], s1_sem.at[0, c], r1_sem.at[0, c],
                device_id={"sec": sec_at(yy, x)}, device_id_type=MESH).start()
        for d in sorted(range(1, NX), key=lambda d: far(d, NX)):
            xx = lax.rem(x + d, NX)
            pltpu.make_async_remote_copy(
                ybuf.at[c, :, xx, pl.ds(half, half)], b1.at[c, d - 1], s1_sem.at[1, c], r1_sem.at[1, c],
                device_id={"sec": sec_at(y, xx)}, device_id_type=MESH).start()

    def by_target_at_once(c):
        wait_for(zrecv.at[c, pl.ds(0, W - 1)], zr_sem.at[pairs + c])
        arrived = zrecv[c].reshape(K, COLS)
        for dy in sorted(range(NY), key=lambda d: far(d, NY)):
            yy = lax.rem(y + dy, NY)
            first = pl.multiple_of(yy * block_rows, block_rows)
            part = jnp.dot(
                onehot[pl.ds(first, block_rows), :], arrived, preferred_element_type=jnp.float32)
            ybuf[c, yy] = part.astype(jnp.bfloat16).reshape(NX, NB * SUB, COLS)
            for dx in sorted(range(NX), key=lambda d: far(d, NX)):
                if dx or dy:
                    xx = lax.rem(x + dx, NX)
                    pltpu.make_async_remote_copy(
                        ybuf.at[c, yy, xx], direct.at[dy * NX + dx - 1], d_sem.at[0], d_sem.at[1],
                        device_id={"sec": sec_at(yy, xx)}, device_id_type=MESH).start()

    def add_direct(c):
        wait_for(direct, d_sem.at[1])
        total = ybuf[c, y, x].astype(jnp.float32)
        for n in range(SEC - 1):
            total = total + direct[n].astype(jnp.float32)
        fin[c] = total

    def one_axis(c):
        wait_for(a1.at[c], r1_sem.at[0, c])
        total = ybuf[c, y, :, :half, :].astype(jnp.float32)
        for n in range(NY - 1):
            total = total + a1[c, n].astype(jnp.float32)
        a2s[c] = total.astype(jnp.bfloat16)
        for d in sorted(range(1, NX), key=lambda d: far(d, NX)):
            xx = lax.rem(x + d, NX)
            pltpu.make_async_remote_copy(
                a2s.at[c, xx], a2.at[c, d - 1], s2_sem.at[0, c], r2_sem.at[0, c],
                device_id={"sec": sec_at(y, xx)}, device_id_type=MESH).start()
        wait_for(b1.at[c], r1_sem.at[1, c])
        total = ybuf[c, :, x, half:, :].astype(jnp.float32)
        for n in range(NX - 1):
            total = total + b1[c, n].astype(jnp.float32)
        b2s[c] = total.astype(jnp.bfloat16)
        for d in sorted(range(1, NY), key=lambda d: far(d, NY)):
            yy = lax.rem(y + d, NY)
            pltpu.make_async_remote_copy(
                b2s.at[c, yy], b2.at[c, d - 1], s2_sem.at[1, c], r2_sem.at[1, c],
                device_id={"sec": sec_at(yy, x)}, device_id_type=MESH).start()

    def other_axis(c):
        wait_for(a2.at[c], r2_sem.at[0, c])
        wait_for(b2.at[c], r2_sem.at[1, c])
        for own, others, place, at in ((a2s, a2, x, 0), (b2s, b2, y, half)):
            total = own[c, place].astype(jnp.float32)
            for n in range(others.shape[1]):
                total = total + others[c, n].astype(jnp.float32)
            fin[c, at:at + half, :] = total

    def place_items():
        wait_for(xrecv.at[:, pl.ds(0, SEC - 1)], xr_sem.at[1])
        for n in range(W * XG // 2):
            part = jnp.dot(
                xhot[...], xrecv[n].reshape(SEC * 2 * SUB, COLS), preferred_element_type=jnp.float32
            ).astype(jnp.bfloat16)
            for e in range(2):
                at = 2 * n + e
                to, first = at // XG, at % XG * NB * SUB
                xplaced[to % 2, to // 2, first:first + NB * SUB, :] = part[e * NB * SUB:(e + 1) * NB * SUB]
        pltpu.make_async_remote_copy(
            xplaced.at[1 - core], xcore, xs_sem.at[2], xr_sem.at[2],
            device_id={"term": w + 1 - 2 * core}, device_id_type=MESH).start()

    def add_cores():
        wait_for(xcore, xr_sem.at[2])
        xsum[...] = (xplaced[core].astype(jnp.float32) + xcore[...].astype(jnp.float32)).astype(jnp.bfloat16)
        for d in sorted(range(1, W // 2), key=lambda d: far(d, W // 2)):
            peer = lax.rem(z + d, W // 2)
            pltpu.make_async_remote_copy(
                xsum.at[peer], xlast.at[d - 1], xs_sem.at[3], xr_sem.at[3],
                device_id={"term": peer * 2 + core}, device_id_type=MESH).start()

    def step_of(t, carry):
        @pl.when(t == G)
        def _():
            place_items()

        @pl.when(t == G + 1)
        def _():
            add_cores()

        @pl.when(t < C - 1)
        def _():
            by_target(t)

        @pl.when(t == C - 1)
        def _():
            by_target_at_once(C - 1)

        @pl.when((t >= 1) & (t < C))
        def _():
            one_axis(t - 1)

        @pl.when(t >= 2)
        def _():
            other_axis(t - 2)

        return carry

    lax.fori_loop(0, C + 1, step_of, 0)
    add_direct(C - 1)

    wait_for(xlast, xr_sem.at[3])
    total = xsum[z].astype(jnp.float32)
    for n in range(W // 2 - 1):
        total = total + xlast[n].astype(jnp.float32)
    fin[C:] = total.reshape(XG, NB * SUB, COLS)

    row_id = lax.broadcasted_iota(jnp.int32, (rows, BS), 0) + w * rows
    col_id = lax.broadcasted_iota(jnp.int32, (rows, BS), 1)
    for j in range(NB):
        keep = (row_id < dims[0, j]) & (col_id < dims[1, j])
        total = jnp.concatenate([
            jnp.concatenate([
                fin[q * G + g, j * SUB:(j + 1) * SUB, :] for q in range(BS // COLS)], axis=1)
            for g in range(G)], axis=0)
        out[j] = jnp.where(keep, total, 0.0).astype(out.dtype)

    wait_for(mrecv.at[pl.ds(0, W - 1)], mesh_sems.at[0])
    for p in range(pairs):
        part = pl.ds(p * 2 * SUB, 2 * SUB)
        wait_for(zsend.at[pl.ds(0, G), pl.ds(0, W - 1), part], zs_sem.at[p])

    def sent(c, carry):
        @pl.when(c >= G)
        def _():
            wait_for(zsend.at[c, pl.ds(0, W - 1)], zs_sem.at[pairs + c])

        @pl.when(c < C - 1)
        def _():
            wait_for(a1.at[c], s1_sem.at[0, c])
            wait_for(b1.at[c], s1_sem.at[1, c])
            wait_for(a2.at[c], s2_sem.at[0, c])
            wait_for(b2.at[c], s2_sem.at[1, c])

        return carry

    lax.fori_loop(0, C, sent, 0)
    wait_for(direct, d_sem.at[0])
    wait_for(xmrecv.at[pl.ds(0, SEC - 1)], xs_sem.at[0])
    wait_for(xsend.at[pl.ds(0, SEC - 1)], xs_sem.at[1])
    wait_for(xcore, xs_sem.at[2])
    wait_for(xlast, xs_sem.at[3])


def shards(W, SEC, psi, left_env, right_env, targets, selected, block_dims):
    NB, BS, _ = psi.shape
    NX = math.isqrt(SEC)
    NY = SEC // NX
    rows = BS // W
    C = BS // COLS * (rows // SUB) - XG
    pairs_here = W * XG // 2
    R6 = ITEMS * SUB
    half = NB * SUB // 2
    bf16, f32, i32 = jnp.bfloat16, jnp.float32, jnp.int32
    dma = pltpu.SemaphoreType.DMA
    hbm = pl.BlockSpec(memory_space=pltpu.HBM)
    return pl.pallas_call(
        functools.partial(kernel, W, NY, NX),
        out_shape=pltpu.VMEM((NB, rows, BS), bf16),
        in_specs=[hbm] * 6,
        out_specs=pl.BlockSpec(memory_space=pltpu.VMEM),
        scratch_shapes=[
            pltpu.SMEM((1, NB), i32),
            pltpu.SMEM((1, NB), i32),
            pltpu.SMEM((2, NB), i32),
            pltpu.VMEM((NB, BS, BS), bf16),
            pltpu.VMEM((NB, 2, BS, BS), bf16),
            pltpu.VMEM((NB, 2, BS, COLS), bf16),
            pltpu.VMEM((NB, 2, BS, BS - COLS), bf16),
            pltpu.VMEM((ITEMS, BS, 2 * BS), bf16),
            pltpu.VMEM((C, W, R6, COLS), bf16),
            pltpu.VMEM((C, W, R6, COLS), bf16),
            pltpu.VMEM((1, 128), i32),
            pltpu.VMEM((W, 1, 128), i32),
            pltpu.VMEM((SEC * NB * SUB, W * R6), bf16),
            pltpu.VMEM((C, NY, NX, NB * SUB, COLS), bf16),
            pltpu.VMEM((C - 1, NY - 1, NX, half, COLS), bf16),
            pltpu.VMEM((C - 1, NX - 1, NY, half, COLS), bf16),
            pltpu.VMEM((C - 1, NX, half, COLS), bf16),
            pltpu.VMEM((C - 1, NY, half, COLS), bf16),
            pltpu.VMEM((C - 1, NX - 1, half, COLS), bf16),
            pltpu.VMEM((C - 1, NY - 1, half, COLS), bf16),
            pltpu.VMEM((C + XG, NB * SUB, COLS), f32),
            pltpu.VMEM((SEC - 1, NB * SUB, COLS), bf16),
            pltpu.VMEM((SEC, 1, 128), i32),
            pltpu.VMEM((SEC, 1, 128), i32),
            pltpu.VMEM((ITEMS, pairs_here, 2 * SUB, COLS), bf16),
            pltpu.VMEM((SEC, pairs_here, 2 * SUB, COLS), bf16),
            pltpu.VMEM((pairs_here, SEC, 2 * SUB, COLS), bf16),
            pltpu.VMEM((2 * NB * SUB, SEC * 2 * SUB), bf16),
            pltpu.VMEM((2, W // 2, XG * NB * SUB, COLS), bf16),
            pltpu.VMEM((W // 2, XG * NB * SUB, COLS), bf16),
            pltpu.VMEM((W // 2, XG * NB * SUB, COLS), bf16),
            pltpu.VMEM((W // 2 - 1, XG * NB * SUB, COLS), bf16),
            dma((3,)), dma((7,)), dma((2,)), dma((ITEMS // 2 + C,)), dma((ITEMS // 2 + C,)),
            dma((2, C - 1)), dma((2, C - 1)), dma((2, C - 1)), dma((2, C - 1)), dma((4,)), dma((4,)), dma((2,)),
        ],
        compiler_params=pltpu.CompilerParams(
            collective_id=0, has_side_effects=True, vmem_limit_bytes=54 * 2**20),
        cost_estimate=pl.CostEstimate(flops=8 * 10**9, bytes_accessed=12 * 10**6, transcendentals=0),
        name="davidson",
    )(targets, selected, block_dims.T, psi, left_env, right_env)


def solution(mesh):
    W, SEC = mesh.shape["term"], mesh.shape["sec"]
    return jax.shard_map(
        functools.partial(shards, W, SEC),
        mesh=mesh,
        in_specs=(
            P("sec", None, None),
            P("term", None, "sec", None, None),
            P("term", None, "sec", None, None),
            P("term", "sec"),
            P("term", "sec"),
            P("sec", None),
        ),
        out_specs=P("sec", "term", None),
        check_vma=False,
    )
```
